128 devices in a mesh: ep: 16 (over x, z), etp: 8 (over y, core).
Axes of the slice: x: 4, y: 4, z: 4, core: 2. Of those that a mesh axis runs over, the one named last changes fastest.
Arguments:
- tokens: bfloat16 [1024, 7168], P('ep', 'etp'), may hold values from -6 to 6
- cotangent: bfloat16 [1024, 7168], P('ep', 'etp'), may hold values from -6 to 6
- expert_ids: int32 [1024, 8], P('ep'), may hold values from 0 to 15, all different within a row; in each aligned block of 64 rows (0 to 63, 64 to 127, ...) at most 40 rows name the same one
- routing_gate_weight: bfloat16 [1024, 8], P('ep'), may hold values from 0.049804688 to 1
- gate_projection_weight: bfloat16 [16, 7168, 2048], P('ep', None, 'etp'), may hold values from -0.0625 to 0.0625
- up_weight: bfloat16 [16, 7168, 2048], P('ep', None, 'etp'), may hold values from -0.0625 to 0.0625
- down_weight: bfloat16 [16, 2048, 7168], P('ep', 'etp'), may hold values from -0.125 to 0.125
Outputs:
- input_grad: bfloat16 [1024, 7168], P('ep', 'etp')
- gate_grad: float32 [1024, 8], P('ep')
- w_gate_grad: bfloat16 [16, 7168, 2048], P('ep', None, 'etp')
- w_up_grad: bfloat16 [16, 7168, 2048], P('ep', None, 'etp')
- w_down_grad: bfloat16 [16, 2048, 7168], P('ep', 'etp')
The draws below stay inside these ranges and needn't reach their ends.
Inputs may be any that keep to these rules, and one draw needn't show every extreme that they name: `expert_ids`: each row names 8 different experts. Among the rows of one index of ep no expert is named more than 40 times, a bound that some block reaches.
All inputs are finite; a program needn't handle non-finite values.
Results may differ from the reference program's by a relative error of at most 0.019.
Values may be sent and summed in bfloat16 or wider, within the bound.
No kernel may reach another device: no remote copies, remote signals or barrier semaphores. Data moves between devices by JAX's collectives and lax.ppermute only.
A program may use at most 192 MiB of HBM per device.

```python
import math
import jax
import jax.numpy as jnp
import numpy as np
from jax import lax

D = 7168
FF = 2048
TOP = 8
TOK_EP = 64
TOKENS = 1024
EXPERT_COUNT = 16
EXPERT_ROOM = 40
N_EP = 16
N_ETP = 8


def block_levels(own_key, shape, split, smallest, high):
    def one(position, parts):
        steps = jax.random.uniform(jax.random.fold_in(jax.random.fold_in(own_key, 6), position), (parts,), jnp.float32, smallest / len(split), high / len(split))
        return jnp.repeat(jnp.exp(steps), shape[position] // parts).reshape((-1,) + (1,) * (len(shape) - position - 1))

    loudness = one(*split[0])
    for cut in split[1:]:
        loudness = loudness * one(*cut)
    return loudness


def shared_out(stream_key, own, number, rows, count, top, reach, lean):
    order = jax.random.permutation(stream_key, count)
    crowded, usual = portions_of(count, rows * top, reach, lean, True), portions_of(count, rows * top, reach, lean, False)
    places = jnp.arange(count)

    def named(tallies, rotation):
        used = int((tallies > 0).sum())
        fixed = max(1, used // 4)
        moved = fixed + (places - fixed + rotation * (used - fixed)) % max(1, count - fixed)
        return jnp.zeros((count,), jnp.int32).at[order[jnp.where(places < fixed, places, moved)]].set(jnp.asarray(tallies, jnp.int32))

    tallies = jnp.where(number % 4 == 0, named(crowded, number // 4), named(usual, number - number // 4 - 1))
    mixed = jax.random.permutation(jax.random.fold_in(own, 3), count)
    donor, receiver = mixed[0:count // 2 * 2:2], mixed[1:count // 2 * 2:2]
    room = jnp.minimum(tallies[donor] - 1, reach - tallies[receiver]) // 2
    room = jnp.where((donor == order[0]) | (receiver == order[0]) | (tallies[receiver] == 0), 0, jnp.maximum(room, 0))
    moved = jax.random.randint(jax.random.fold_in(own, 4), (count // 2,), 0, 1 << 20) % (room + 1)
    tallies = tallies.at[donor].add(-moved).at[receiver].add(moved)
    labels = jnp.searchsorted(jnp.cumsum(tallies), jnp.arange(rows * top), side="right").astype(jnp.int32)
    table = labels.reshape(top, rows).T
    table = table[jax.random.permutation(jax.random.fold_in(own, 1), rows)]
    rotation = jax.random.randint(jax.random.fold_in(own, 2), (rows, 1), 0, top)
    return jnp.take_along_axis(table, (jnp.arange(top)[None, :] + rotation) % top, axis=1)


def portions_of(amount, total, reach, lean, full):
    weights = [(1 << 20) // math.isqrt(rank ** lean) + 1 for rank in range(1, amount + 1)]
    largest = reach if full else min(reach, max(-(-total // amount), total * weights[0] // sum(weights)))
    least = 1 if total - largest >= amount - 1 else 0
    counts, surplus = [largest] + [least] * (amount - 1), total - largest - least * (amount - 1)
    while surplus > 0:
        free = [i for i in range(1, amount) if counts[i] < largest] or [i for i in range(1, amount) if counts[i] < reach]
        pool, budget = sum([weights[i] for i in free]), surplus
        for i in free:
            more = min(reach - counts[i], max(1, budget * weights[i] // pool), surplus)
            counts[i] = counts[i] + more
            surplus = surplus - more
    return np.array(counts)


def normal_values(rng, dims, scale, bound, pieces=(), kind=jnp.bfloat16):
    entries = scale * jax.random.normal(rng, dims, jnp.float32)
    if pieces:
        entries = entries * block_levels(rng, dims, pieces, -0.22, 0.18)
    return jnp.clip(entries, -bound, bound).astype(kind)


def setup_inputs(seed: int = 0) -> dict:
    arg_keys = jax.random.split(jax.random.key(seed), 8)
    tokens = normal_values(arg_keys[0], (TOKENS, D), 1.0, 6.0, ((0, 16), (1, 8)))
    cotangent = normal_values(arg_keys[1], (TOKENS, D), 1.0, 6.0, ((0, 16), (1, 8)))
    expert_ids_keys = jax.random.split(jax.random.fold_in(arg_keys[2], 1), TOKENS // TOK_EP)
    expert_ids_turns = jax.random.permutation(jax.random.fold_in(arg_keys[2], 3), TOKENS // TOK_EP)
    expert_ids = jax.vmap(lambda own, number: shared_out(jax.random.fold_in(arg_keys[2], 2), own, number, TOK_EP, EXPERT_COUNT, TOP, EXPERT_ROOM, 1))(expert_ids_keys, expert_ids_turns).reshape((TOKENS, TOP))
    routing_gate_weight = jnp.clip(jnp.exp(math.log(1.0) - 2.9996462 * jax.random.uniform(arg_keys[3], (TOKENS, TOP), jnp.float32) ** block_levels(arg_keys[3], (TOKENS, TOP), ((0, 16),), -0.2, 0.2)), 0.049804688, 1.0).astype(jnp.bfloat16)
    gate_projection_weight = normal_values(arg_keys[4], (EXPERT_COUNT, D, FF), D ** -0.5, 0.0625, ((0, 16), (2, 8)))
    up_weight = normal_values(arg_keys[5], (EXPERT_COUNT, D, FF), D ** -0.5, 0.0625, ((0, 16), (2, 8)))
    down_weight = normal_values(arg_keys[6], (EXPERT_COUNT, FF, D), FF ** -0.5, 0.125, ((0, 16), (1, 8)))
    return dict(tokens=tokens, cotangent=cotangent, expert_ids=expert_ids, routing_gate_weight=routing_gate_weight, gate_projection_weight=gate_projection_weight, up_weight=up_weight, down_weight=down_weight)


def pair_ranks(expert_ids):
    blocks = expert_ids.reshape(N_EP, TOK_EP * TOP)
    onehot = (blocks[:, :, None] == jnp.arange(EXPERT_COUNT, dtype=jnp.int32)[None, None, :]).astype(jnp.int32)
    before = jnp.cumsum(onehot, axis=1) - onehot
    return jnp.sum(before * onehot, axis=2).reshape(TOKENS, TOP).astype(jnp.int32)


def expert_gradient_pass(packed):
    xe, dye, ge, wg, wu, wd = packed
    a = jnp.dot(xe, wg, preferred_element_type=jnp.float32)
    b = jnp.dot(xe, wu, preferred_element_type=jnp.float32)
    sig = jax.nn.sigmoid(a)
    s = a * sig
    h = s * b
    gf = ge.astype(jnp.float32)[:, None]
    hs = (gf * h).astype(jnp.bfloat16)
    down_weight_gradient = jnp.dot(hs.T, dye, preferred_element_type=jnp.float32).astype(jnp.bfloat16)
    raw = jnp.dot(dye, wd.T, preferred_element_type=jnp.float32)
    slotted_gate = jnp.sum(h * raw, axis=1)
    dh = gf * raw
    da = (dh * b * sig * (1.0 + a * (1.0 - sig))).astype(jnp.bfloat16)
    db = (dh * s).astype(jnp.bfloat16)
    gate_weight_gradient = jnp.dot(xe.T, da, preferred_element_type=jnp.float32).astype(jnp.bfloat16)
    up_weight_gradient = jnp.dot(xe.T, db, preferred_element_type=jnp.float32).astype(jnp.bfloat16)
    width = FF // N_ETP
    total = jnp.zeros((xe.shape[0], D), jnp.float32)
    for group in range(N_ETP):
        lo = group * width
        part = jnp.dot(da[:, lo:lo + width], wg[:, lo:lo + width].T, preferred_element_type=jnp.float32)
        part = part + jnp.dot(db[:, lo:lo + width], wu[:, lo:lo + width].T, preferred_element_type=jnp.float32)
        total = total + lax.optimization_barrier(part.astype(jnp.bfloat16)).astype(jnp.float32)
    return gate_weight_gradient, up_weight_gradient, down_weight_gradient, total, slotted_gate


def reference(tokens, cotangent, expert_ids, routing_gate_weight, gate_projection_weight, up_weight, down_weight):
    rank = pair_ranks(expert_ids)
    block = (jnp.arange(TOKENS, dtype=jnp.int32) // TOK_EP).astype(jnp.int32)
    target_slot = (expert_ids * (N_EP * EXPERT_ROOM) + block[:, None] * EXPERT_ROOM + rank).reshape(-1).astype(jnp.int32)
    source = jnp.repeat(jnp.arange(TOKENS, dtype=jnp.int32), TOP)
    slot_positions = EXPERT_COUNT * N_EP * EXPERT_ROOM
    input_buffer = jnp.zeros((slot_positions, D), jnp.bfloat16).at[target_slot].set(tokens[source]).reshape(EXPERT_COUNT, N_EP * EXPERT_ROOM, D)
    output_gradient_buffer = jnp.zeros((slot_positions, D), jnp.bfloat16).at[target_slot].set(cotangent[source]).reshape(EXPERT_COUNT, N_EP * EXPERT_ROOM, D)
    gate_buffer = jnp.zeros((slot_positions,), jnp.bfloat16).at[target_slot].set(routing_gate_weight.reshape(-1)).reshape(EXPERT_COUNT, N_EP * EXPERT_ROOM)
    gate_weight_gradient, up_weight_gradient, down_weight_gradient, slotted_input, slotted_gate = lax.map(expert_gradient_pass, (input_buffer, output_gradient_buffer, gate_buffer, gate_projection_weight, up_weight, down_weight))
    picked = slotted_input.reshape(slot_positions, D)[target_slot].reshape(TOKENS, TOP, D)
    input_grad = jnp.sum(picked, axis=1).astype(jnp.bfloat16)
    gate_grad = slotted_gate.reshape(slot_positions)[target_slot].reshape(TOKENS, TOP)
    return input_grad, gate_grad, gate_weight_gradient, up_weight_gradient, down_weight_gradient
```

```python
import jax
import jax.numpy as jnp
from jax import lax
from jax.experimental import pallas as pl
from jax.experimental.pallas import tpu as pltpu
from jax.sharding import PartitionSpec as P


def nt_dot(left, right):
    return lax.dot_general(left, right, (((1,), (1,)), ((), ())), preferred_element_type=jnp.float32)


def input_part_kernel(da_ref, db_ref, wg_ref, wu_ref, out_ref):
    part = nt_dot(da_ref[...], wg_ref[...]) + nt_dot(db_ref[...], wu_ref[...])
    out_ref[0] = part.astype(jnp.bfloat16)


def input_parts(da, db, wg, wu, slices):
    rows, hidden = da.shape
    cols = wg.shape[0] // slices
    whole = pl.BlockSpec((rows, hidden), lambda j: (0, 0))
    block = pl.BlockSpec((cols, hidden), lambda j: (j, 0))
    return pl.pallas_call(
        input_part_kernel,
        grid=(slices,),
        in_specs=[whole, whole, block, block],
        out_specs=pl.BlockSpec((1, rows, cols), lambda j: (j, 0, 0)),
        out_shape=jax.ShapeDtypeStruct((slices, rows, cols), jnp.bfloat16),
        compiler_params=pltpu.CompilerParams(vmem_limit_bytes=40 * 2**20),
    )(da, db, wg, wu)


def local(
    tokens,
    cotangent,
    expert_ids,
    routing_gate_weight,
    gate_projection_weight,
    up_weight,
    down_weight,
):
    ep_count = lax.axis_size("ep")
    tok_rows = tokens.shape[0]
    choose = expert_ids.shape[1]
    capacity = min(tok_rows, tok_rows * choose * 5 // (4 * ep_count))
    width = down_weight.shape[2]
    flat_ids = expert_ids.reshape(-1)
    onehot = (flat_ids[:, None] == jnp.arange(ep_count, dtype=jnp.int32)[None, :]).astype(jnp.int32)
    before = jnp.cumsum(onehot, axis=0) - onehot
    rank = jnp.sum(before * onehot, axis=1)
    target_slot = flat_ids * capacity + rank
    source = jnp.repeat(jnp.arange(tok_rows, dtype=jnp.int32), choose)
    slot_positions = ep_count * capacity
    slice_cols = tokens.shape[1]
    send_x = (
        jnp.zeros((slot_positions, slice_cols), jnp.bfloat16)
        .at[target_slot]
        .set(tokens[source])
        .reshape(ep_count, capacity, slice_cols)
    )
    send_dy = (
        jnp.zeros((slot_positions, slice_cols), jnp.bfloat16)
        .at[target_slot]
        .set(cotangent[source])
        .reshape(ep_count, capacity, slice_cols)
    )
    send_g = (
        jnp.zeros((slot_positions,), jnp.bfloat16)
        .at[target_slot]
        .set(routing_gate_weight.reshape(-1))
        .reshape(ep_count, capacity)
    )
    recv_x, recv_dy, recv_g = (
        lax.all_to_all(send_x, "ep", split_axis=0, concat_axis=0, tiled=True),
        lax.all_to_all(send_dy, "ep", split_axis=0, concat_axis=0, tiled=True),
        lax.all_to_all(send_g, "ep", split_axis=0, concat_axis=0, tiled=True),
    )
    full_x, full_dy = (
        lax.all_gather(recv_x, "etp", axis=2, tiled=True),
        lax.all_gather(recv_dy, "etp", axis=2, tiled=True),
    )
    xe = full_x.reshape(slot_positions, width)
    dye = full_dy.reshape(slot_positions, width)
    wg = gate_projection_weight[0]
    wu = up_weight[0]
    wd = down_weight[0]
    a = jnp.dot(xe, wg, preferred_element_type=jnp.float32)
    b = jnp.dot(xe, wu, preferred_element_type=jnp.float32)
    sig = jax.nn.sigmoid(a)
    s = a * sig
    h = s * b
    gf = recv_g.reshape(slot_positions).astype(jnp.float32)[:, None]
    hs = (gf * h).astype(jnp.bfloat16)
    down_weight_gradient = jnp.dot(hs.T, dye, preferred_element_type=jnp.float32).astype(
        jnp.bfloat16
    )
    raw = jnp.dot(dye, wd.T, preferred_element_type=jnp.float32)
    gate_local = jnp.sum(h * raw, axis=1)
    dh = gf * raw
    da = (dh * b * sig * (1.0 + a * (1.0 - sig))).astype(jnp.bfloat16)
    db = (dh * s).astype(jnp.bfloat16)
    gate_weight_gradient = jnp.dot(xe.T, da, preferred_element_type=jnp.float32).astype(
        jnp.bfloat16
    )
    up_weight_gradient = jnp.dot(xe.T, db, preferred_element_type=jnp.float32).astype(jnp.bfloat16)
    parts = input_parts(da, db, wg, wu, width // slice_cols)
    slotted_gate = lax.psum(gate_local, "etp").reshape(ep_count, capacity)
    share = lax.psum_scatter(parts, "etp", scatter_dimension=0, tiled=False).reshape(
        ep_count, capacity, slice_cols
    )
    back, gate_back = (
        lax.all_to_all(share, "ep", split_axis=0, concat_axis=0, tiled=True),
        lax.all_to_all(slotted_gate, "ep", split_axis=0, concat_axis=0, tiled=True),
    )
    picked = back.reshape(slot_positions, slice_cols)[target_slot].reshape(
        tok_rows, choose, slice_cols
    )
    input_grad = jnp.sum(picked.astype(jnp.float32), axis=1).astype(jnp.bfloat16)
    gate_grad = gate_back.reshape(slot_positions)[target_slot].reshape(tok_rows, choose)
    return (
        input_grad,
        gate_grad,
        gate_weight_gradient[None],
        up_weight_gradient[None],
        down_weight_gradient[None],
    )


def solution(mesh):
    in_specs = (
        P("ep", "etp"),
        P("ep", "etp"),
        P("ep", None),
        P("ep", None),
        P("ep", None, "etp"),
        P("ep", None, "etp"),
        P("ep", "etp", None),
    )
    out_specs = (
        P("ep", "etp"),
        P("ep", None),
        P("ep", None, "etp"),
        P("ep", None, "etp"),
        P("ep", "etp", None),
    )
    return jax.shard_map(local, mesh=mesh, in_specs=in_specs, out_specs=out_specs, check_vma=False)
```

```python
import functools

import jax
import jax.numpy as jnp
from jax import lax
from jax.experimental import pallas as pl
from jax.experimental.pallas import tpu as pltpu
from jax.sharding import Mesh, PartitionSpec as P

BF, F32 = jnp.bfloat16, jnp.float32
ROWS, COLS, HID, PAD, ROOM, TAIL = 640, 896, 256, 128, 40, 16
SWAP = [(0, 1), (1, 0)]
ANY = pl.BlockSpec(memory_space=pl.ANY)
VMEM = pl.BlockSpec(memory_space=pltpu.VMEM)
SMEM = pl.BlockSpec(memory_space=pltpu.SMEM)
HBM = pl.BlockSpec(memory_space=pltpu.HBM)


def partner(i, core, step):
    return i ^ 1 if core == step else 3 - i


MEET = tuple(
    [(2 * i + c, 2 * partner(i, c, step) + c) for i in range(4) for c in range(2)] for step in range(2)
)


def meet(v, step):
    return lax.ppermute(v, ("y", "core"), MEET[step])


def swap(v):
    return lax.ppermute(v, "core", SWAP)


def nn(left, right):
    return jnp.dot(left, right, preferred_element_type=F32)


def nt(left, right):
    return lax.dot_general(left, right, (((1,), (1,)), ((), ())), preferred_element_type=F32)


def tn(left, right):
    return lax.dot_general(left, right, (((0,), (0,)), ((), ())), preferred_element_type=F32)


def sds(shape, dtype=BF):
    return jax.ShapeDtypeStruct(shape, dtype)


def call(kernel, ins, outs, scratch=(), us=1, mib=24):
    return pl.pallas_call(
        kernel,
        in_specs=ins,
        out_specs=[spec for spec, _ in outs],
        out_shape=[shape for _, shape in outs],
        scratch_shapes=scratch,
        compiler_params=pltpu.CompilerParams(vmem_limit_bytes=mib * 2**20),
        cost_estimate=pl.CostEstimate(flops=0, bytes_accessed=int(us * 3.6e6), transcendentals=0),
    )


def dispatch_kernel(ids, gates, x, dy, send_x, send_dy, onehot):
    expert = lax.broadcasted_iota(jnp.int32, (16, 64), 0)
    named = jnp.zeros((16, 64), F32)
    weight = jnp.zeros((16, 64), F32)
    for k in range(8):
        here = ids[k : k + 1, :] == expert
        named = named + jnp.where(here, 1.0, 0.0)
        weight = weight + jnp.where(here, gates[k : k + 1, :], 0.0)
    one, two = (lax.broadcasted_iota(jnp.int32, (64, 64), axis) for axis in range(2))
    rank = nn(named.astype(BF), jnp.where(one < two, 1.0, 0.0).astype(BF)).astype(jnp.int32)
    slot = lax.broadcasted_iota(jnp.int32, (ROOM, 64), 0)
    picks, sums = [], []
    for e in range(16):
        pick = jnp.where((rank[e : e + 1, :] == slot) & (named[e : e + 1, :] > 0.0), 1.0, 0.0)
        picks.append(pick)
        sums.append(jnp.sum(pick * weight[e : e + 1, :], axis=1, keepdims=True))
    pick = jnp.concatenate(picks, axis=0).astype(BF)
    onehot[...] = pick
    send_x[...] = nn(pick, x[...]).astype(BF)
    send_dy[:, :COLS] = nn(pick, dy[...]).astype(BF)
    send_dy[:, COLS:] = jnp.broadcast_to(jnp.concatenate(sums, axis=0), (ROWS, PAD)).astype(BF)


def dispatch(ids, gates, x, dy):
    outs = [(VMEM, sds((ROWS, COLS))), (VMEM, sds((ROWS, COLS + PAD))), (VMEM, sds((ROWS, 64)))]
    return call(dispatch_kernel, [VMEM] * 4, outs, us=4)(ids, gates, x, dy)


def combine_kernel(back, onehot, ids, *refs):
    grad, gate = refs[-2:]
    pick = onehot[...]
    grad[...] = tn(pick, back[:, :COLS]).astype(BF)
    sums = tn(pick, back[:, COLS:])
    lane = lax.broadcasted_iota(jnp.int32, (64, PAD), 1)
    total = jnp.zeros((64, PAD), F32)
    for k in range(8):
        mine = ids[:, k : k + 1]
        value = jnp.sum(jnp.where((lane == mine) | (lane == mine + 64), sums, 0.0), axis=1, keepdims=True)
        total = total + jnp.where(lane == k, value, 0.0)
    gate[...] = total[:, :8]


def combine(back, onehot, ids):
    outs = [(VMEM, sds((64, COLS))), (VMEM, sds((64, 8), F32))]
    return call(combine_kernel, [VMEM] * 3, outs, us=3)(back, onehot, ids)


def block(ref, i):
    return ref.at[pl.ds(pl.multiple_of(i * COLS, COLS), COLS), :]


def column_block(ref, i):
    return ref.at[:, pl.ds(pl.multiple_of(i * COLS, COLS), COLS)]


def hidden_steps(first, place, xs, wg, wu, x, g, u, a, b, sems):
    def copies(n, src):
        i = place[first + n]
        return [
            pltpu.make_async_copy(src, x.at[n], sems.at[0, n]),
            pltpu.make_async_copy(block(wg, i), g.at[n], sems.at[1, n]),
            pltpu.make_async_copy(block(wu, i), u.at[n], sems.at[2, n]),
        ]

    for n in range(len(xs)):
        for copy in copies(n, xs[n]):
            copy.start()

    @pl.loop(0, len(xs))
    def _(n):
        for copy in copies(n, xs[0]):
            copy.wait()
        a[...] += nn(x[n], g[n])
        b[...] += nn(x[n], u[n])


def first_hidden_kernel(n, place, *refs):
    xs, (wg, wu, a, b, x, g, u, sems) = refs[:n], refs[n:]
    a[...] = jnp.zeros_like(a)
    b[...] = jnp.zeros_like(b)
    hidden_steps(0, place, xs, wg, wu, x, g, u, a, b, sems)


def hidden_kernel(n, place, *refs):
    xs, (wg, wu, a0, b0, s_ref, slope_ref, h_ref, x, g, u, a, b, sems) = refs[:n], refs[n:]
    a[...] = a0[...]
    b[...] = b0[...]
    hidden_steps(8 - n, place, xs, wg, wu, x, g, u, a, b, sems)
    for lo in range(0, ROWS, 128):
        rows = pl.ds(lo, 128)
        av, bv = a[rows, :], b[rows, :]
        sig = jax.nn.sigmoid(av)
        s = av * sig
        s_ref[rows, :] = s
        h_ref[rows, :] = s * bv
        slope_ref[rows, :] = bv * sig * (1.0 + av * (1.0 - sig))


def hidden_scratch(n):
    return [pltpu.VMEM((n, ROWS, COLS), BF)] + [pltpu.VMEM((n, COLS, HID), BF)] * 2


def first_hidden(place, xs, wg, wu):
    n = len(xs)
    scratch = hidden_scratch(n) + [pltpu.SemaphoreType.DMA((3, n))]
    outs = [(VMEM, sds((ROWS, HID), F32))] * 2
    kernel = functools.partial(first_hidden_kernel, n)
    return call(kernel, [SMEM] + [HBM] * (n + 2), outs, scratch, us=9, mib=32)(place, *xs, wg, wu)


def hidden(place, xs, wg, wu, a, b):
    n = len(xs)
    scratch = hidden_scratch(n) + [pltpu.VMEM((ROWS, HID), F32)] * 2 + [pltpu.SemaphoreType.DMA((3, n))]
    outs = [(VMEM, sds((ROWS, HID), F32))] * 3
    ins = [SMEM] + [HBM] * (n + 2) + [VMEM] * 2
    return call(functools.partial(hidden_kernel, n), ins, outs, scratch, us=5)(place, *xs, wg, wu, a, b)


def after(v, *later):
    return pl.pallas_call(
        lambda *refs: None,
        in_specs=[HBM] + [ANY] * len(later),
        out_specs=HBM,
        out_shape=sds(v.shape, v.dtype),
        input_output_aliases={0: 0},
    )(v, *later)


def raw_steps(ks, place, dys, wd, dy, w, acc, sems):
    def copies(n, src):
        return [
            pltpu.make_async_copy(src, dy.at[n], sems.at[0, n]),
            pltpu.make_async_copy(column_block(wd, place[ks[0] + n]), w.at[n], sems.at[1, n]),
        ]

    for n in range(len(ks)):
        for copy in copies(n, dys[n]):
            copy.start()

    @pl.loop(0, len(ks))
    def _(n):
        for copy in copies(n, dys[0]):
            copy.wait()
        acc[...] += nt(dy[n], w[n])


def first_raw_kernel(ks, place, *refs):
    n = len(ks)
    dys, (wd, _, raw, dy, w, sems) = refs[:n], refs[n:]
    raw[...] = jnp.zeros_like(raw)
    raw_steps(ks, place, dys, wd, dy, w, raw, sems)


def raw_scratch(n):
    return [pltpu.VMEM((n, ROWS, COLS), BF), pltpu.VMEM((n, HID, COLS), BF), pltpu.SemaphoreType.DMA((2, n))]


def first_raw(ks, place, dys, wd, later):
    kernel = functools.partial(first_raw_kernel, ks)
    outs = [(VMEM, sds((ROWS, HID), F32))]
    return call(kernel, [SMEM] + [HBM] * (len(ks) + 1) + [ANY], outs, raw_scratch(len(ks)), us=5)(place, *dys, wd, later)[0]


def gradient_kernel(ks, place, *refs):
    n = len(ks)
    dys = refs[:n]
    wd, first, s_ref, slope_ref, h_ref, gate, dab, hs, sums, acc, dy, w, sems = refs[n:]
    acc[...] = first[...]
    raw_steps(ks, place, dys, wd, dy, w, acc, sems)
    sums[...] = jnp.zeros_like(sums)
    for i in range(ROWS // 128):
        rows = pl.ds(128 * i, 128)
        g, raw, h = gate[rows, 0:1].astype(F32), acc[rows, :], h_ref[rows, :]
        total = jnp.sum(h * raw, axis=1, keepdims=True)
        sums[0:1, pl.ds(128 * i, 128)] = jnp.broadcast_to(total, (128, 128)).T[0:1, :]
        dh = g * raw
        dab[rows, :HID] = (dh * slope_ref[rows, :]).astype(BF)
        dab[rows, HID:] = (dh * s_ref[rows, :]).astype(BF)
        hs[rows, :] = (g * h).astype(BF)


def gradients(ks, place, dys, wd, first, s, slope, h, gate):
    outs = [(VMEM, sds((ROWS, 2 * HID))), (VMEM, sds((ROWS, HID))), (VMEM, sds((TAIL, COLS), F32))]
    kernel = functools.partial(gradient_kernel, ks)
    scratch = [pltpu.VMEM((ROWS, HID), F32)] + raw_scratch(len(ks))
    ins = [SMEM] + [HBM] * (len(ks) + 1) + [VMEM] * 5
    return call(kernel, ins, outs, scratch, us=6)(place, *dys, wd, first, s, slope, h, gate)


def input_kernel(k, place, dab, sums, wg, wu, *refs):
    sib, own, g, u, sems = refs[-5:]

    def copies(j, i):
        return [
            pltpu.make_async_copy(block(wg, i), g.at[j], sems.at[0, j]),
            pltpu.make_async_copy(block(wu, i), u.at[j], sems.at[1, j]),
        ]

    for j, out in enumerate((sib, own)):
        for copy in copies(j, place[2 * k + 1 - j]):
            copy.start()
    for j, out in enumerate((sib, own)):
        for copy in copies(j, place[2 * k + 1 - j]):
            copy.wait()
        out[:ROWS, :] = (nt(dab[:, :HID], g[j]) + nt(dab[:, HID:], u[j])).astype(BF)
        out[ROWS:, :] = sums[...].astype(BF)


def input_part(k, place, dab, sums, wg, wu, *later):
    scratch = [pltpu.VMEM((2, COLS, HID), BF)] * 2 + [pltpu.SemaphoreType.DMA((2, 2))]
    outs = [(VMEM, sds((ROWS + TAIL, COLS)))] * 2
    ins = [SMEM, VMEM, VMEM, HBM, HBM] + [ANY] * len(later)
    return call(functools.partial(input_kernel, k), ins, outs, scratch, us=3.5)(place, dab, sums, wg, wu, *later)


def column_gradient_kernel(place, *refs):
    xs, (dab, g_out, u_out, x, g, u, sems) = refs[:8], refs[8:]

    def load(k, src):
        return pltpu.make_async_copy(src, x.at[k], sems.at[0, k])

    def stores(k):
        i = place[k]
        return [
            pltpu.make_async_copy(g.at[k], block(g_out, i), sems.at[1, k]),
            pltpu.make_async_copy(u.at[k], block(u_out, i), sems.at[2, k]),
        ]

    for k in range(8):
        load(k, xs[k]).start()

    @pl.loop(0, 8)
    def _(k):
        load(k, xs[0]).wait()
        value = tn(x[k], dab[...])
        g[k] = value[:, :HID].astype(BF)
        u[k] = value[:, HID:].astype(BF)
        for copy in stores(k):
            copy.start()

    @pl.loop(0, 8)
    def _(k):
        for copy in stores(k):
            copy.wait()


def column_gradients(place, xs, dab):
    scratch = [pltpu.VMEM((8, ROWS, COLS), BF)] + [pltpu.VMEM((8, COLS, HID), BF)] * 2
    scratch += [pltpu.SemaphoreType.DMA((3, 8))]
    outs = [(HBM, sds((8 * COLS, HID)))] * 2
    return call(column_gradient_kernel, [SMEM] + [HBM] * 8 + [VMEM], outs, scratch, us=10, mib=32)(place, *xs, dab)


def row_gradient_kernel(place, *refs):
    dys, (hs, out, dy, d, sems) = refs[:8], refs[8:]

    def load(k, src):
        return pltpu.make_async_copy(src, dy.at[k], sems.at[0, k])

    def store(k):
        return pltpu.make_async_copy(d.at[k], column_block(out, place[k]), sems.at[1, k])

    for k in range(8):
        load(k, dys[k]).start()
    hst = hs[...].T

    @pl.loop(0, 8)
    def _(k):
        load(k, dys[0]).wait()
        d[k] = nn(hst, dy[k]).astype(BF)
        store(k).start()

    @pl.loop(0, 8)
    def _(k):
        store(k).wait()


def row_gradient(place, dys, hs):
    scratch = [pltpu.VMEM((8, ROWS, COLS), BF), pltpu.VMEM((8, HID, COLS), BF), pltpu.SemaphoreType.DMA((2, 8))]
    outs = [(HBM, sds((HID, 8 * COLS)))]
    return call(row_gradient_kernel, [SMEM] + [HBM] * 8 + [VMEM], outs, scratch, us=6, mib=24)(place, *dys, hs)[0]


def total_kernel(expert, *refs):
    terms, out = refs[:4], refs[-1]
    lane = lax.broadcasted_iota(jnp.int32, (128, PAD), 1)
    gates = sum(term[ROWS:, :].astype(F32) for term in terms)
    for i in range(ROWS // 128):
        rows = pl.ds(128 * i, 128)
        out[rows, :COLS] = sum(term[rows, :].astype(F32) for term in terms).astype(BF)
        gate = jnp.broadcast_to(gates[0:1, 128 * i : 128 * i + 128], (128, 128)).T
        high = gate.astype(BF).astype(F32)
        spread = jnp.where(lane == expert[0], high, 0.0) + jnp.where(lane == expert[0] + 64, gate - high, 0.0)
        out[rows, COLS:] = spread.astype(BF)


def total(expert, terms, *later):
    outs = [(VMEM, sds((ROWS, COLS + PAD)))]
    ins = [SMEM] + [VMEM] * 4 + [ANY] * len(later)
    return call(total_kernel, ins, outs, us=2)(expert, *terms, *later)[0]


def exchange(v):
    return lax.all_to_all(v.reshape(16, ROOM, -1), ("x", "z"), 0, 0, tiled=True).reshape(ROWS, -1)


def ring(v):
    return [v, meet(v, 0), meet(v, 1)]


def with_swaps(pieces):
    return [v for piece in pieces for v in (piece, swap(piece))]


def add(*terms):
    return sum(term.astype(F32) for term in terms).astype(BF)


def local(tokens, cotangent, ids, gates, wg, wu, wd):
    core, iy = lax.axis_index("core"), lax.axis_index("y")
    expert = (lax.axis_index("x") * 4 + lax.axis_index("z")).astype(jnp.int32).reshape(1)
    ys = [iy, jnp.where(core == 0, iy ^ 1, 3 - iy), jnp.where(core == 0, 3 - iy, iy ^ 1), (iy + 2) % 4]
    place = [2 * ys[k] + core if own else 2 * ys[(0, 2, 1, 3)[k]] + 1 - core for k in range(4) for own in (1, 0)]
    place = jnp.stack(place).astype(jnp.int32)
    wg, wu, wd = wg[0], wu[0], wd[0]

    send_x, send_dy, onehot = dispatch(ids.T, gates.T.astype(F32), tokens, cotangent)
    xs = ring(exchange(send_x))
    last = meet(xs[1], 1)
    xs = with_swaps(xs)
    came = exchange(send_dy)
    gate = came[:, COLS:]
    a, b = first_hidden(place, xs, wg, wu)
    dys = ring(came[:, :COLS])
    dys[1] = after(dys[1], a)
    dy_last = meet(dys[1], 1)
    xs = xs + with_swaps([last])
    dys = with_swaps(dys + [dy_last])

    s, slope, h = hidden(place, xs[6:], wg, wu, a, b)
    raw = first_raw(range(6), place, dys[:6], wd, h)
    dab, hs, sums = gradients(range(6, 8), place, dys[6:], wd, raw, s, slope, h, gate)

    def part(k, *later):
        sib, own = input_part(k, place, dab, sums, wg, wu, *later)
        return own, swap(sib)

    opposite = add(*part(3))
    second = part(2)
    first = part(1, opposite)
    opposite = meet(opposite, 1)
    near = add(*second)
    own = part(0, near)
    near = meet(near, 1)
    rest = meet(add(*first, opposite), 0)

    down_grad = row_gradient(place, dys, hs)
    gate_grad, up_grad = column_gradients(place, xs, dab)
    share = total(expert, (*own, near, rest), down_grad, gate_grad)
    input_grad, slot_grad = combine(exchange(share), onehot, ids)
    return input_grad, slot_grad, gate_grad[None], up_grad[None], down_grad[None]


def solution(mesh):
    torus = Mesh(mesh.devices.reshape(4, 4, 4, 2), ("x", "z", "y", "core"))
    ep, etp = ("x", "z"), ("y", "core")
    in_specs = (
        P(ep, etp),
        P(ep, etp),
        P(ep, None),
        P(ep, None),
        P(ep, None, etp),
        P(ep, None, etp),
        P(ep, etp, None),
    )
    out_specs = (P(ep, etp), P(ep, None), P(ep, None, etp), P(ep, None, etp), P(ep, etp, None))
    return jax.shard_map(local, mesh=torus, in_specs=in_specs, out_specs=out_specs, check_vma=False)
```

```python
import functools

import jax
import jax.numpy as jnp
from jax import lax
from jax.experimental import pallas as pl
from jax.experimental.pallas import tpu as pltpu
from jax.sharding import Mesh, PartitionSpec as P

BF, F32 = jnp.bfloat16, jnp.float32
ROWS, COLS, HID, PAD, ROOM, TAIL = 640, 896, 256, 128, 40, 16
SWAP = [(0, 1), (1, 0)]
ANY = pl.BlockSpec(memory_space=pl.ANY)
MOST = 61
RATE = 3e10
VMEM = pl.BlockSpec(memory_space=pltpu.VMEM)
SMEM = pl.BlockSpec(memory_space=pltpu.SMEM)
HBM = pl.BlockSpec(memory_space=pltpu.HBM)


def partner(i, core, step):
    return i ^ 1 if core == step else 3 - i


MEET = tuple(
    [(2 * i + c, 2 * partner(i, c, step) + c) for i in range(4) for c in range(2)] for step in range(2)
)


def meet(v, step):
    return lax.ppermute(v, ("y", "core"), MEET[step])


def swap(v):
    return lax.ppermute(v, "core", SWAP)


def nn(left, right):
    return jnp.dot(left, right, preferred_element_type=F32)


def nt(left, right):
    return lax.dot_general(left, right, (((1,), (1,)), ((), ())), preferred_element_type=F32)


def tn(left, right):
    return lax.dot_general(left, right, (((0,), (0,)), ((), ())), preferred_element_type=F32)


def sds(shape, dtype=BF):
    return jax.ShapeDtypeStruct(shape, dtype)


def call(kernel, ins, outs, scratch=(), us=1, mib=24):
    return pl.pallas_call(
        kernel,
        in_specs=ins,
        out_specs=[spec for spec, _ in outs],
        out_shape=[shape for _, shape in outs],
        scratch_shapes=scratch,
        compiler_params=pltpu.CompilerParams(vmem_limit_bytes=mib * 2**20),
        cost_estimate=pl.CostEstimate(flops=int(us * RATE), bytes_accessed=10000, transcendentals=0),
    )


def dispatch_kernel(ids, gates, x_ref, dy_ref, send_x, send_dy, onehot, x, dy, sems):
    copies = [pltpu.make_async_copy(x_ref, x, sems.at[0]), pltpu.make_async_copy(dy_ref, dy, sems.at[1])]
    for copy in copies:
        copy.start()
    expert = lax.broadcasted_iota(jnp.int32, (16, 64), 0)
    named = jnp.zeros((16, 64), F32)
    weight = jnp.zeros((16, 64), F32)
    for k in range(8):
        here = ids[k : k + 1, :] == expert
        named = named + jnp.where(here, 1.0, 0.0)
        weight = weight + jnp.where(here, gates[k : k + 1, :], 0.0)
    one, two = (lax.broadcasted_iota(jnp.int32, (64, 64), axis) for axis in range(2))
    rank = nn(named.astype(BF), jnp.where(one < two, 1.0, 0.0).astype(BF)).astype(jnp.int32)
    slot = lax.broadcasted_iota(jnp.int32, (ROOM, 64), 0)
    picks, sums = [], []
    for e in range(16):
        pick = jnp.where((rank[e : e + 1, :] == slot) & (named[e : e + 1, :] > 0.0), 1.0, 0.0)
        picks.append(pick)
        sums.append(jnp.sum(pick * weight[e : e + 1, :], axis=1, keepdims=True))
    pick = jnp.concatenate(picks, axis=0).astype(BF)
    onehot[...] = pick
    for copy in copies:
        copy.wait()
    send_x[...] = nn(pick, x[...]).astype(BF)
    send_dy[:, :COLS] = nn(pick, dy[...]).astype(BF)
    send_dy[:, COLS:] = jnp.broadcast_to(jnp.concatenate(sums, axis=0), (ROWS, PAD)).astype(BF)


def dispatch(ids, gates, x, dy):
    outs = [(VMEM, sds((ROWS, COLS))), (VMEM, sds((ROWS, COLS + PAD))), (VMEM, sds((ROWS, 64)))]
    scratch = [pltpu.VMEM((64, COLS), BF)] * 2 + [pltpu.SemaphoreType.DMA((2,))]
    return call(dispatch_kernel, [VMEM] * 2 + [HBM] * 2, outs, scratch, us=4)(ids, gates, x, dy)


def combine_kernel(back, onehot, ids, *refs):
    grad, gate = refs[-2:]
    pick = onehot[...]
    grad[...] = tn(pick, back[:, :COLS]).astype(BF)
    sums = tn(pick, back[:, COLS:])
    lane = lax.broadcasted_iota(jnp.int32, (64, PAD), 1)
    total = jnp.zeros((64, PAD), F32)
    for k in range(8):
        mine = ids[:, k : k + 1]
        value = jnp.sum(jnp.where((lane == mine) | (lane == mine + 64), sums, 0.0), axis=1, keepdims=True)
        total = total + jnp.where(lane == k, value, 0.0)
    gate[...] = total[:, :8]


def combine(back, onehot, ids, later):
    outs = [(VMEM, sds((64, COLS))), (VMEM, sds((64, 8), F32))]
    return call(combine_kernel, [VMEM] * 3 + [ANY], outs, us=3)(back, onehot, ids, later)


def block(ref, i):
    return ref.at[pl.ds(pl.multiple_of(i * COLS, COLS), COLS), :]


def column_block(ref, i):
    return ref.at[:, pl.ds(pl.multiple_of(i * COLS, COLS), COLS)]


def pack_kernel(*refs):
    weights, (columns, rows, w, d, sems) = refs[:6], refs[6:]
    loads, stores = [], []
    for j in range(6):
        buffer, out = (w.at[j], columns.at[:, pl.ds(HID * j, HID)]) if j < 4 else (d.at[j - 4], rows.at[pl.ds(HID * (j - 4), HID), :])
        loads.append(pltpu.make_async_copy(weights[j], buffer, sems.at[0, j]))
        stores.append(pltpu.make_async_copy(buffer, out, sems.at[1, j]))
    for copy in loads:
        copy.start()
    for load, store in zip(loads, stores):
        load.wait()
        store.start()
    for copy in stores:
        copy.wait()


def pack(*weights):
    scratch = [pltpu.VMEM((4, 8 * COLS, HID), BF), pltpu.VMEM((2, HID, 8 * COLS), BF), pltpu.SemaphoreType.DMA((2, 6))]
    outs = [(HBM, sds((8 * COLS, 4 * HID))), (HBM, sds((2 * HID, 8 * COLS)))]
    return call(pack_kernel, [HBM] * 6, outs, scratch, us=13, mib=MOST)(*weights)


def hidden_steps(ks, place, xs, ws, x, w, acc, sems):
    def copies(n, src):
        i = place[ks[0] + n]
        first = pltpu.make_async_copy(src, x.at[n], sems.at[1, n])
        return [first, pltpu.make_async_copy(block(ws, i), w.at[n], sems.at[0, n])]

    for n in range(len(ks)):
        for copy in copies(n, xs[n]):
            copy.start()

    @pl.loop(0, len(ks))
    def _(n):
        for copy in copies(n, xs[0]):
            copy.wait()
        acc[...] += nn(x[n], w[n])


def hidden_scratch(n):
    return [pltpu.VMEM((n, ROWS, COLS), BF), pltpu.VMEM((n, COLS, 4 * HID), BF), pltpu.SemaphoreType.DMA((2, n))]


def first_hidden_kernel(ks, place, *refs):
    n = len(ks)
    ws, acc, x, w, sems = refs[n:]
    acc[...] = jnp.zeros_like(acc)
    hidden_steps(ks, place, refs[:n], ws, x, w, acc, sems)


def first_hidden(ks, place, xs, ws):
    outs = [(VMEM, sds((ROWS, 4 * HID), F32))]
    kernel = functools.partial(first_hidden_kernel, ks)
    ins = [SMEM] + [HBM] * (len(ks) + 1)
    return call(kernel, ins, outs, hidden_scratch(len(ks)), us=8, mib=MOST)(place, *xs, ws)[0]


def raw_steps(ks, place, dys, ws, dy, w, acc, sems):
    def copies(n, src):
        i = place[ks[0] + n]
        first = pltpu.make_async_copy(src, dy.at[n], sems.at[1, n])
        return [first, pltpu.make_async_copy(column_block(ws, i), w.at[n], sems.at[0, n])]

    for n in range(len(ks)):
        for copy in copies(n, dys[n]):
            copy.start()

    @pl.loop(0, len(ks))
    def _(n):
        for copy in copies(n, dys[0]):
            copy.wait()
        acc[...] += nt(dy[n], w[n])


def raw_scratch(n):
    return [pltpu.VMEM((n, ROWS, COLS), BF), pltpu.VMEM((n, 2 * HID, COLS), BF), pltpu.SemaphoreType.DMA((2, n))]


def middle_kernel(place, x_last, d0, d1, d2, *refs):
    ws, ds, first, keep, send, raw, acc, x, w, sems, dy, v, dsems = refs
    acc[...] = first[...]
    hidden_steps(range(3, 4), place, [x_last], ws, x, w, acc, sems)
    keep[...] = acc[:, : 2 * HID]
    send[...] = acc[:, 2 * HID :]
    raw[...] = jnp.zeros_like(raw)
    raw_steps(range(3), place, [d0, d1, d2], ds, dy, v, raw, dsems)


def middle(place, x_last, dys, ws, ds, first):
    outs = [(VMEM, sds((ROWS, 2 * HID), F32))] * 3
    scratch = [pltpu.VMEM((ROWS, 4 * HID), F32)] + hidden_scratch(1) + raw_scratch(3)
    ins = [SMEM] + [HBM] * 6 + [VMEM]
    return call(middle_kernel, ins, outs, scratch, us=12, mib=MOST)(place, x_last, *dys, ws, ds, first)


def activation_kernel(keep, came, s_ref, slope_ref, h_ref):
    for lo in range(0, ROWS, 128):
        rows = pl.ds(lo, 128)
        ab = keep[rows, :] + came[rows, :]
        av, bv = ab[:, :HID], ab[:, HID:]
        sig = jax.nn.sigmoid(av)
        s = av * sig
        s_ref[rows, :] = s
        h_ref[rows, :] = s * bv
        slope_ref[rows, :] = bv * sig * (1.0 + av * (1.0 - sig))


def activation(keep, came):
    return call(activation_kernel, [VMEM] * 2, [(VMEM, sds((ROWS, HID), F32))] * 3)(keep, came)


def raw_kernel(ks, place, *refs):
    n = len(ks)
    ws, first, keep, send, acc, dy, w, sems = refs[n:]
    acc[...] = first[...]
    raw_steps(ks, place, refs[:n], ws, dy, w, acc, sems)
    keep[...] = acc[:, :HID]
    send[...] = acc[:, HID:]


def raw_rest(ks, place, dys, ws, first):
    outs = [(VMEM, sds((ROWS, HID), F32))] * 2
    scratch = [pltpu.VMEM((ROWS, 2 * HID), F32)] + raw_scratch(len(ks))
    ins = [SMEM] + [HBM] * (len(ks) + 1) + [VMEM]
    return call(functools.partial(raw_kernel, ks), ins, outs, scratch, us=3, mib=58)(place, *dys, ws, first)


def gradient_kernel(keep, came, s_ref, slope_ref, h_ref, gate, dab, hs):
    sums = []
    for i in range(ROWS // 128):
        rows = pl.ds(128 * i, 128)
        g, raw, h = gate[rows, 0:1].astype(F32), keep[rows, :] + came[rows, :], h_ref[rows, :]
        value = jnp.sum(h * raw, axis=1, keepdims=True)
        sums.append(jnp.broadcast_to(value, (128, 128)).T[0:1, :])
        dh = g * raw
        dab[rows, :HID] = (dh * slope_ref[rows, :]).astype(BF)
        dab[rows, HID:] = (dh * s_ref[rows, :]).astype(BF)
        hs[rows, :] = (g * h).astype(BF)
    tail = [jnp.concatenate(sums[:4], axis=1), jnp.concatenate([sums[4], jnp.zeros((1, 384), F32)], axis=1)]
    dab[ROWS:, :] = jnp.concatenate(tail + [jnp.zeros((TAIL - 2, 512), F32)], axis=0).astype(BF)


def gradients(keep, came, s, slope, h, gate):
    outs = [(VMEM, sds((ROWS + TAIL, 2 * HID))), (VMEM, sds((ROWS, HID)))]
    return call(gradient_kernel, [VMEM] * 6, outs)(keep, came, s, slope, h, gate)


def input_kernel(k, place, own, other, *refs):
    ws, (out, w, grads, sem) = refs[0], refs[-4:]
    copy = pltpu.make_async_copy(block(ws, place[k]), w, sem)
    copy.start()
    grads[:, : 2 * HID], grads[:, 2 * HID :] = own[:ROWS, :], other[:ROWS, :]
    tail = own[ROWS:, :].astype(F32) + other[ROWS:, :].astype(F32)
    row = jnp.concatenate([tail[0:1, :], tail[1:2, :384]], axis=1)
    out[ROWS:, :] = jnp.concatenate([row, jnp.zeros((TAIL - 1, COLS), F32)], axis=0).astype(BF)
    copy.wait()
    out[:ROWS, :] = nt(grads[...], w[...]).astype(BF)


def input_part(k, place, own, other, ws, *later):
    scratch = [pltpu.VMEM((COLS, 4 * HID), BF), pltpu.VMEM((ROWS, 4 * HID), BF), pltpu.SemaphoreType.DMA]
    outs = [(VMEM, sds((ROWS + TAIL, COLS)))]
    ins = [SMEM, VMEM, VMEM, HBM] + [ANY] * len(later)
    return call(functools.partial(input_kernel, k), ins, outs, scratch, us=4, mib=51)(place, own, other, ws, *later)[0]


def stream(refs, buffer, sems):
    def load(k, src):
        return pltpu.make_async_copy(src, buffer.at[k], sems.at[k])

    for k, ref in enumerate(refs):
        load(k, ref).start()
    return lambda k: load(k, refs[0]).wait()


def other_gradient_kernel(*refs):
    xs, dys, (dab, hs, _, columns, rows, x, dy, c, r, xsems, dsems, sems) = refs[:4], refs[4:8], refs[8:]
    x_ready, dy_ready = stream(xs, x, xsems), stream(dys, dy, dsems)

    def stores(k):
        return [
            pltpu.make_async_copy(c.at[k], columns.at[k], sems.at[0, k]),
            pltpu.make_async_copy(r.at[k], rows.at[k], sems.at[1, k]),
        ]

    hst = hs[...].T

    @pl.loop(0, 4)
    def _(k):
        x_ready(k)
        c[k] = tn(x[k], dab[:ROWS, :]).astype(BF)
        dy_ready(k)
        r[k] = nn(hst, dy[k]).astype(BF)
        for copy in stores(k):
            copy.start()

    @pl.loop(0, 4)
    def _(k):
        for copy in stores(k):
            copy.wait()


PIECES = [pltpu.VMEM((4, ROWS, COLS), BF)] * 2 + [pltpu.VMEM((4, COLS, 2 * HID), BF), pltpu.VMEM((4, HID, COLS), BF)]


def other_gradients(xs, dys, dab, hs, later):
    scratch = PIECES + [pltpu.SemaphoreType.DMA((4,))] * 2 + [pltpu.SemaphoreType.DMA((2, 4))]
    outs = [(HBM, sds((4, COLS, 2 * HID))), (HBM, sds((4, HID, COLS)))]
    ins = [HBM] * 8 + [VMEM] * 2 + [ANY]
    return call(other_gradient_kernel, ins, outs, scratch, us=10, mib=MOST)(*xs, *dys, dab, hs, later)


def own_gradient_kernel(place, other_place, *refs):
    xs, dys, refs = refs[:4], refs[4:8], refs[8:]
    dab, hs, columns, rows, _, g, u, d, token, x, dy, c, r, c_in, r_in, xsems, dsems, isems, sems = refs
    token[...] = jnp.zeros_like(token)
    x_ready, dy_ready = stream(xs, x, xsems), stream(dys, dy, dsems)

    def arrivals(k):
        return [
            pltpu.make_async_copy(columns.at[k], c_in.at[k], isems.at[0, k]),
            pltpu.make_async_copy(rows.at[k], r_in.at[k], isems.at[1, k]),
        ]

    def stores(i, k, cols, part, row):
        return [
            pltpu.make_async_copy(cols.at[k, :, pl.ds(0, HID)], block(g, i), sems.at[row, k]),
            pltpu.make_async_copy(cols.at[k, :, pl.ds(HID, HID)], block(u, i), sems.at[row + 1, k]),
            pltpu.make_async_copy(part.at[k], column_block(d, i), sems.at[row + 2, k]),
        ]

    for k in range(4):
        for copy in arrivals(k):
            copy.start()
    hst = hs[...].T

    @pl.loop(0, 4)
    def _(k):
        x_ready(k)
        c[k] = tn(x[k], dab[:ROWS, :]).astype(BF)
        dy_ready(k)
        r[k] = nn(hst, dy[k]).astype(BF)
        for copy in stores(place[k], k, c, r, 0):
            copy.start()
        for copy in arrivals(k):
            copy.wait()
        for copy in stores(other_place[k], k, c_in, r_in, 3):
            copy.start()

    @pl.loop(0, 4)
    def _(k):
        for copy in stores(place[k], k, c, r, 0) + stores(other_place[k], k, c_in, r_in, 3):
            copy.wait()


def own_gradients(place, other_place, xs, dys, dab, hs, columns, rows, later):
    scratch = PIECES + PIECES[2:] + [pltpu.SemaphoreType.DMA((4,))] * 2
    scratch += [pltpu.SemaphoreType.DMA((2, 4)), pltpu.SemaphoreType.DMA((6, 4))]
    outs = [(HBM, sds((8 * COLS, HID)))] * 2 + [(HBM, sds((HID, 8 * COLS))), (VMEM, sds((8, 128), F32))]
    ins = [SMEM] * 2 + [HBM] * 8 + [VMEM] * 2 + [HBM] * 2 + [ANY]
    kernel = call(own_gradient_kernel, ins, outs, scratch, us=12, mib=MOST)
    return kernel(place, other_place, *xs, *dys, dab, hs, columns, rows, later)


def total_kernel(expert, *refs):
    terms, out = refs[:3], refs[-1]
    lane = lax.broadcasted_iota(jnp.int32, (128, PAD), 1)
    gates = sum(term[ROWS:, :].astype(F32) for term in terms)
    for i in range(ROWS // 128):
        rows = pl.ds(128 * i, 128)
        out[rows, :COLS] = sum(term[rows, :].astype(F32) for term in terms).astype(BF)
        gate = jnp.broadcast_to(gates[0:1, 128 * i : 128 * i + 128], (128, 128)).T
        high = gate.astype(BF).astype(F32)
        spread = jnp.where(lane == expert[0], high, 0.0) + jnp.where(lane == expert[0] + 64, gate - high, 0.0)
        out[rows, COLS:] = spread.astype(BF)


def total(expert, terms, *later):
    outs = [(VMEM, sds((ROWS, COLS + PAD)))]
    ins = [SMEM] + [VMEM] * 3 + [ANY] * len(later)
    return call(total_kernel, ins, outs)(expert, *terms, *later)[0]


def after(v, *later):
    return pl.pallas_call(
        lambda *refs: None,
        in_specs=[HBM] + [ANY] * len(later),
        out_specs=HBM,
        out_shape=sds(v.shape, v.dtype),
        input_output_aliases={0: 0},
    )(v, *later)


def exchange(v):
    return lax.all_to_all(v.reshape(16, ROOM, -1), ("x", "z"), 0, 0, tiled=True).reshape(ROWS, -1)


def ring(v):
    return [v, meet(v, 0), meet(v, 1)]


def add(*terms):
    return sum(term.astype(F32) for term in terms).astype(BF)


def local(tokens, cotangent, ids, gates, wg, wu, wd):
    core, iy = lax.axis_index("core"), lax.axis_index("y")
    expert = (lax.axis_index("x") * 4 + lax.axis_index("z")).astype(jnp.int32).reshape(1)
    ys = [iy, jnp.where(core == 0, iy ^ 1, 3 - iy), jnp.where(core == 0, 3 - iy, iy ^ 1), (iy + 2) % 4]
    place = jnp.stack([2 * y + core for y in ys]).astype(jnp.int32)
    other_place = jnp.stack([2 * ys[k] + 1 - core for k in (0, 2, 1, 3)]).astype(jnp.int32)
    wg, wu, wd = wg[0], wu[0], wd[0]

    send_x, send_dy, onehot = dispatch(ids.T, gates.T.astype(F32), tokens, cotangent)
    ws = (wg, wu, swap(wg), swap(wu))
    ds = (wd, swap(wd))
    xs = ring(after(exchange(send_x), ws[2], ws[3], ds[1]))
    x_last = meet(xs[1], 1)
    came = exchange(after(send_dy, xs[0]))
    gate = came[:, COLS:]
    dys = ring(came[:, :COLS])
    dys[1] = after(dys[1], dys[2])
    dy_last = meet(dys[1], 1)

    ws, ds = pack(*ws, *ds)
    first = first_hidden(range(3), place, xs, ws)
    keep, send, raw = middle(place, x_last, dys, ws, ds, first)
    s, slope, h = activation(keep, swap(send))
    keep, send = raw_rest(range(3, 4), place, [dy_last], ds, raw)
    dab, hs = gradients(keep, swap(send), s, slope, h, gate)
    dab_other, hs_other = swap(dab), swap(hs)

    def part(k, *later):
        return input_part(k, place, dab, dab_other, ws, *later)

    opposite = part(3)
    near = part(2, opposite)
    own = part(1, near)
    opposite, near = meet(opposite, 1), meet(near, 1)
    own = add(own, opposite)
    rest = meet(own, 0)
    xs, dys = xs + [x_last], dys + [dy_last]
    columns, rows = other_gradients(xs, dys, dab_other, hs_other, own)
    columns, rows = swap(columns), swap(rows)
    share = total(expert, (part(0, own), near, rest))
    gate_grad, up_grad, down_grad, done = own_gradients(place, other_place, xs, dys, dab, hs, columns, rows, share)
    input_grad, slot_grad = combine(exchange(share), onehot, ids, done)
    return input_grad, slot_grad, gate_grad[None], up_grad[None], down_grad[None]


def solution(mesh):
    torus = Mesh(mesh.devices.reshape(4, 4, 4, 2), ("x", "z", "y", "core"))
    ep, etp = ("x", "z"), ("y", "core")
    in_specs = (
        P(ep, etp),
        P(ep, etp),
        P(ep, None),
        P(ep, None),
        P(ep, None, etp),
        P(ep, None, etp),
        P(ep, etp, None),
    )
    out_specs = (P(ep, etp), P(ep, None), P(ep, None, etp), P(ep, None, etp), P(ep, etp, None))
    return jax.shard_map(local, mesh=torus, in_specs=in_specs, out_specs=out_specs, check_vma=False)
```

```python
import functools

import jax
import jax.numpy as jnp
from jax import lax
from jax.experimental import pallas as pl
from jax.experimental.pallas import tpu as pltpu
from jax.sharding import Mesh, PartitionSpec as P

BF, F32 = jnp.bfloat16, jnp.float32
ROWS, COLS, HID, PAD, ROOM, TAIL = 640, 896, 256, 128, 40, 16
SWAP = [(0, 1), (1, 0)]
ANY = pl.BlockSpec(memory_space=pl.ANY)
MOST = 61
DY_CUT = 512
DY_REST = 896 - DY_CUT
RATE = 3e10
VMEM = pl.BlockSpec(memory_space=pltpu.VMEM)
SMEM = pl.BlockSpec(memory_space=pltpu.SMEM)
HBM = pl.BlockSpec(memory_space=pltpu.HBM)


def partner(i, core, step):
    return i ^ 1 if core == step else 3 - i


MEET = tuple(
    [(2 * i + c, 2 * partner(i, c, step) + c) for i in range(4) for c in range(2)] for step in range(2)
)


def meet(v, step):
    return lax.ppermute(v, ("y", "core"), MEET[step])


def swap(v):
    return lax.ppermute(v, "core", SWAP)


def nn(left, right):
    return jnp.dot(left, right, preferred_element_type=F32)


def nt(left, right):
    return lax.dot_general(left, right, (((1,), (1,)), ((), ())), preferred_element_type=F32)


def tn(left, right):
    return lax.dot_general(left, right, (((0,), (0,)), ((), ())), preferred_element_type=F32)


def sds(shape, dtype=BF):
    return jax.ShapeDtypeStruct(shape, dtype)


def call(kernel, ins, outs, scratch=(), us=1, mib=24):
    return pl.pallas_call(
        kernel,
        in_specs=ins,
        out_specs=[spec for spec, _ in outs],
        out_shape=[shape for _, shape in outs],
        scratch_shapes=scratch,
        compiler_params=pltpu.CompilerParams(vmem_limit_bytes=mib * 2**20),
        cost_estimate=pl.CostEstimate(flops=int(us * RATE), bytes_accessed=10000, transcendentals=0),
    )


def dispatch_kernel(ids, gates, x, send_x, onehot, weights):
    expert = lax.broadcasted_iota(jnp.int32, (16, 64), 0)
    named = jnp.zeros((16, 64), F32)
    weight = jnp.zeros((16, 64), F32)
    for k in range(8):
        here = ids[k : k + 1, :] == expert
        named = named + jnp.where(here, 1.0, 0.0)
        weight = weight + jnp.where(here, gates[k : k + 1, :], 0.0)
    one, two = (lax.broadcasted_iota(jnp.int32, (64, 64), axis) for axis in range(2))
    rank = nn(named.astype(BF), jnp.where(one < two, 1.0, 0.0).astype(BF)).astype(jnp.int32)
    slot = lax.broadcasted_iota(jnp.int32, (ROOM, 64), 0)
    picks, sums = [], []
    for e in range(16):
        pick = jnp.where((rank[e : e + 1, :] == slot) & (named[e : e + 1, :] > 0.0), 1.0, 0.0)
        picks.append(pick)
        sums.append(jnp.sum(pick * weight[e : e + 1, :], axis=1, keepdims=True))
    pick = jnp.concatenate(picks, axis=0).astype(BF)
    onehot[...] = pick
    send_x[...] = nn(pick, x[...]).astype(BF)
    weights[...] = jnp.broadcast_to(jnp.concatenate(sums, axis=0), (ROWS, PAD)).astype(BF)


def dispatch(ids, gates, x):
    outs = [(VMEM, sds((ROWS, COLS))), (VMEM, sds((ROWS, 64))), (VMEM, sds((ROWS, PAD)))]
    return call(dispatch_kernel, [VMEM] * 3, outs, us=3)(ids, gates, x)


def second_dispatch_kernel(onehot, weights, dy, *refs):
    rests, out = refs[:4], refs[4]
    pick = onehot[...]
    out[:, :DY_CUT] = nn(pick, dy[:, :DY_CUT]).astype(BF)
    for k in range(4):
        lo = DY_CUT + DY_REST * k
        out[:, lo : lo + DY_REST] = nn(pick, rests[k][...]).astype(BF)
    out[:, -PAD:] = weights[...]


def second_dispatch(onehot, weights, dy, rests):
    outs = [(VMEM, sds((ROWS, DY_CUT + 4 * DY_REST + PAD)))]
    return call(second_dispatch_kernel, [VMEM] * 7, outs, us=3)(onehot, weights, dy, *rests)[0]


def combine_kernel(back, onehot, ids, *refs):
    grad, gate = refs[-2:]
    pick = onehot[...]
    grad[...] = tn(pick, back[:, :COLS]).astype(BF)
    sums = tn(pick, back[:, COLS:])
    lane = lax.broadcasted_iota(jnp.int32, (64, PAD), 1)
    total = jnp.zeros((64, PAD), F32)
    for k in range(8):
        mine = ids[:, k : k + 1]
        value = jnp.sum(jnp.where((lane == mine) | (lane == mine + 64), sums, 0.0), axis=1, keepdims=True)
        total = total + jnp.where(lane == k, value, 0.0)
    gate[...] = total[:, :8]


def combine(back, onehot, ids, later):
    outs = [(VMEM, sds((64, COLS))), (VMEM, sds((64, 8), F32))]
    return call(combine_kernel, [VMEM] * 3 + [ANY], outs, us=3)(back, onehot, ids, later)


def block(ref, i):
    return ref.at[pl.ds(pl.multiple_of(i * COLS, COLS), COLS), :]


def column_block(ref, i):
    return ref.at[:, pl.ds(pl.multiple_of(i * COLS, COLS), COLS)]


def pack_kernel(*refs):
    weights, (columns, rows, w, d, sems) = refs[:6], refs[6:]
    loads, stores = [], []
    for j in range(6):
        buffer, out = (w.at[j], columns.at[:, pl.ds(HID * j, HID)]) if j < 4 else (d.at[j - 4], rows.at[pl.ds(HID * (j - 4), HID), :])
        loads.append(pltpu.make_async_copy(weights[j], buffer, sems.at[0, j]))
        stores.append(pltpu.make_async_copy(buffer, out, sems.at[1, j]))
    for copy in loads:
        copy.start()
    for load, store in zip(loads, stores):
        load.wait()
        store.start()
    for copy in stores:
        copy.wait()


def pack(*weights):
    scratch = [pltpu.VMEM((4, 8 * COLS, HID), BF), pltpu.VMEM((2, HID, 8 * COLS), BF), pltpu.SemaphoreType.DMA((2, 6))]
    outs = [(HBM, sds((8 * COLS, 4 * HID))), (HBM, sds((2 * HID, 8 * COLS)))]
    return call(pack_kernel, [HBM] * 6, outs, scratch, us=13, mib=MOST)(*weights)


def hidden_steps(ks, place, xs, ws, x, w, acc, sems):
    def copies(n, src):
        i = place[ks[0] + n]
        first = pltpu.make_async_copy(src, x.at[n], sems.at[1, n])
        return [first, pltpu.make_async_copy(block(ws, i), w.at[n], sems.at[0, n])]

    for n in range(len(ks)):
        for copy in copies(n, xs[n]):
            copy.start()

    @pl.loop(0, len(ks))
    def _(n):
        for copy in copies(n, xs[0]):
            copy.wait()
        acc[...] += nn(x[n], w[n])


def hidden_scratch(n):
    return [pltpu.VMEM((n, ROWS, COLS), BF), pltpu.VMEM((n, COLS, 4 * HID), BF), pltpu.SemaphoreType.DMA((2, n))]


def first_hidden_kernel(ks, place, *refs):
    n = len(ks)
    ws, acc, x, w, sems = refs[n:]
    acc[...] = jnp.zeros_like(acc)
    hidden_steps(ks, place, refs[:n], ws, x, w, acc, sems)


def first_hidden(ks, place, xs, ws):
    outs = [(VMEM, sds((ROWS, 4 * HID), F32))]
    kernel = functools.partial(first_hidden_kernel, ks)
    ins = [SMEM] + [HBM] * (len(ks) + 1)
    return call(kernel, ins, outs, hidden_scratch(len(ks)), us=8, mib=MOST)(place, *xs, ws)[0]


def dy_copies(k, ring_part, came, out, sems):
    rest = came.at[:, pl.ds(pl.multiple_of(DY_CUT + DY_REST * k, 128), DY_REST)]
    return [
        pltpu.make_async_copy(ring_part, out.at[:, pl.ds(0, DY_CUT)], sems.at[0]),
        pltpu.make_async_copy(rest, out.at[:, pl.ds(DY_CUT, DY_REST)], sems.at[1]),
    ]


def raw_steps(ks, place, dys, came, ws, dy, w, acc, sems):
    def copies(n, src):
        i = place[ks[0] + n]
        pieces = dy_copies(ks[0] + n, src, came, dy.at[n], sems.at[n])
        return pieces + [pltpu.make_async_copy(column_block(ws, i), w.at[n], sems.at[n, 2])]

    for n in range(len(ks)):
        for copy in copies(n, dys[n]):
            copy.start()

    @pl.loop(0, len(ks))
    def _(n):
        for copy in copies(n, dys[0]):
            copy.wait()
        acc[...] += nt(dy[n], w[n])


def raw_scratch(n):
    return [pltpu.VMEM((n, ROWS, COLS), BF), pltpu.VMEM((n, 2 * HID, COLS), BF), pltpu.SemaphoreType.DMA((n, 3))]


def middle_kernel(place, x_last, d0, d1, d2, came, *refs):
    ws, ds, first, keep, send, raw, acc, x, w, sems, dy, v, dsems = refs
    acc[...] = first[...]
    hidden_steps(range(3, 4), place, [x_last], ws, x, w, acc, sems)
    keep[...] = acc[:, : 2 * HID]
    send[...] = acc[:, 2 * HID :]
    raw[...] = jnp.zeros_like(raw)
    raw_steps(range(3), place, [d0, d1, d2], came, ds, dy, v, raw, dsems)


def middle(place, x_last, dys, came, ws, ds, first):
    outs = [(VMEM, sds((ROWS, 2 * HID), F32))] * 3
    scratch = [pltpu.VMEM((ROWS, 4 * HID), F32)] + hidden_scratch(1) + raw_scratch(3)
    ins = [SMEM] + [HBM] * 7 + [VMEM]
    return call(middle_kernel, ins, outs, scratch, us=12, mib=MOST)(place, x_last, *dys, came, ws, ds, first)


def activation_kernel(keep, came, s_ref, slope_ref, h_ref):
    for lo in range(0, ROWS, 128):
        rows = pl.ds(lo, 128)
        ab = keep[rows, :] + came[rows, :]
        av, bv = ab[:, :HID], ab[:, HID:]
        sig = jax.nn.sigmoid(av)
        s = av * sig
        s_ref[rows, :] = s
        h_ref[rows, :] = s * bv
        slope_ref[rows, :] = bv * sig * (1.0 + av * (1.0 - sig))


def activation(keep, came):
    return call(activation_kernel, [VMEM] * 2, [(VMEM, sds((ROWS, HID), F32))] * 3)(keep, came)


def raw_kernel(ks, place, *refs):
    n = len(ks)
    came, ws, first, keep, send, acc, dy, w, sems = refs[n:]
    acc[...] = first[...]
    raw_steps(ks, place, refs[:n], came, ws, dy, w, acc, sems)
    keep[...] = acc[:, :HID]
    send[...] = acc[:, HID:]


def raw_rest(ks, place, dys, came, ws, first):
    outs = [(VMEM, sds((ROWS, HID), F32))] * 2
    scratch = [pltpu.VMEM((ROWS, 2 * HID), F32)] + raw_scratch(len(ks))
    ins = [SMEM] + [HBM] * (len(ks) + 2) + [VMEM]
    return call(functools.partial(raw_kernel, ks), ins, outs, scratch, us=3, mib=58)(place, *dys, came, ws, first)


def gradient_kernel(keep, came, s_ref, slope_ref, h_ref, gate, dab, hs):
    sums = []
    for i in range(ROWS // 128):
        rows = pl.ds(128 * i, 128)
        g, raw, h = gate[rows, 0:1].astype(F32), keep[rows, :] + came[rows, :], h_ref[rows, :]
        value = jnp.sum(h * raw, axis=1, keepdims=True)
        sums.append(jnp.broadcast_to(value, (128, 128)).T[0:1, :])
        dh = g * raw
        dab[rows, :HID] = (dh * slope_ref[rows, :]).astype(BF)
        dab[rows, HID:] = (dh * s_ref[rows, :]).astype(BF)
        hs[rows, :] = (g * h).astype(BF)
    tail = [jnp.concatenate(sums[:4], axis=1), jnp.concatenate([sums[4], jnp.zeros((1, 384), F32)], axis=1)]
    dab[ROWS:, :] = jnp.concatenate(tail + [jnp.zeros((TAIL - 2, 512), F32)], axis=0).astype(BF)


def gradients(keep, came, s, slope, h, gate):
    outs = [(VMEM, sds((ROWS + TAIL, 2 * HID))), (VMEM, sds((ROWS, HID)))]
    return call(gradient_kernel, [VMEM] * 6, outs)(keep, came, s, slope, h, gate)


def input_kernel(k, place, own, other, *refs):
    ws, (out, w, grads, sem) = refs[0], refs[-4:]
    copy = pltpu.make_async_copy(block(ws, place[k]), w, sem)
    copy.start()
    grads[:, : 2 * HID], grads[:, 2 * HID :] = own[:ROWS, :], other[:ROWS, :]
    tail = own[ROWS:, :].astype(F32) + other[ROWS:, :].astype(F32)
    row = jnp.concatenate([tail[0:1, :], tail[1:2, :384]], axis=1)
    out[ROWS:, :] = jnp.concatenate([row, jnp.zeros((TAIL - 1, COLS), F32)], axis=0).astype(BF)
    copy.wait()
    out[:ROWS, :] = nt(grads[...], w[...]).astype(BF)


def input_part(k, place, own, other, ws, *later):
    scratch = [pltpu.VMEM((COLS, 4 * HID), BF), pltpu.VMEM((ROWS, 4 * HID), BF), pltpu.SemaphoreType.DMA]
    outs = [(VMEM, sds((ROWS + TAIL, COLS)))]
    ins = [SMEM, VMEM, VMEM, HBM] + [ANY] * len(later)
    return call(functools.partial(input_kernel, k), ins, outs, scratch, us=4, mib=51)(place, own, other, ws, *later)[0]


def stream(refs, buffer, sems):
    def load(k, src):
        return pltpu.make_async_copy(src, buffer.at[k], sems.at[k])

    for k, ref in enumerate(refs):
        load(k, ref).start()
    return lambda k: load(k, refs[0]).wait()


def dy_stream(refs, came, buffer, sems):
    for k, ref in enumerate(refs):
        for copy in dy_copies(k, ref, came, buffer.at[k], sems.at[k]):
            copy.start()

    def ready(k):
        for copy in dy_copies(k, refs[0], came, buffer.at[k], sems.at[k]):
            copy.wait()

    return ready


def other_gradient_kernel(*refs):
    xs, dys, (came, dab, hs, _, columns, rows, x, dy, c, r, xsems, dsems, sems) = refs[:4], refs[4:8], refs[8:]
    x_ready, dy_ready = stream(xs, x, xsems), dy_stream(dys, came, dy, dsems)

    def stores(k):
        return [
            pltpu.make_async_copy(c.at[k], columns.at[k], sems.at[0, k]),
            pltpu.make_async_copy(r.at[k], rows.at[k], sems.at[1, k]),
        ]

    hst = hs[...].T

    @pl.loop(0, 4)
    def _(k):
        x_ready(k)
        c[k] = tn(x[k], dab[:ROWS, :]).astype(BF)
        dy_ready(k)
        r[k] = nn(hst, dy[k]).astype(BF)
        for copy in stores(k):
            copy.start()

    @pl.loop(0, 4)
    def _(k):
        for copy in stores(k):
            copy.wait()


PIECES = [pltpu.VMEM((4, ROWS, COLS), BF)] * 2 + [pltpu.VMEM((4, COLS, 2 * HID), BF), pltpu.VMEM((4, HID, COLS), BF)]


def other_gradients(xs, dys, came, dab, hs, later):
    scratch = PIECES + [pltpu.SemaphoreType.DMA((4,)), pltpu.SemaphoreType.DMA((4, 2)), pltpu.SemaphoreType.DMA((2, 4))]
    outs = [(HBM, sds((4, COLS, 2 * HID))), (HBM, sds((4, HID, COLS)))]
    ins = [HBM] * 9 + [VMEM] * 2 + [ANY]
    return call(other_gradient_kernel, ins, outs, scratch, us=10, mib=MOST)(*xs, *dys, came, dab, hs, later)


def own_gradient_kernel(place, other_place, *refs):
    xs, dys, came, refs = refs[:4], refs[4:8], refs[8], refs[9:]
    dab, hs, columns, rows, _, g, u, d, token, x, dy, c, r, c_in, r_in, xsems, dsems, isems, sems = refs
    token[...] = jnp.zeros_like(token)
    x_ready, dy_ready = stream(xs, x, xsems), dy_stream(dys, came, dy, dsems)

    def arrivals(k):
        return [
            pltpu.make_async_copy(columns.at[k], c_in.at[k], isems.at[0, k]),
            pltpu.make_async_copy(rows.at[k], r_in.at[k], isems.at[1, k]),
        ]

    def stores(i, k, cols, part, row):
        return [
            pltpu.make_async_copy(cols.at[k, :, pl.ds(0, HID)], block(g, i), sems.at[row, k]),
            pltpu.make_async_copy(cols.at[k, :, pl.ds(HID, HID)], block(u, i), sems.at[row + 1, k]),
            pltpu.make_async_copy(part.at[k], column_block(d, i), sems.at[row + 2, k]),
        ]

    for k in range(4):
        for copy in arrivals(k):
            copy.start()
    hst = hs[...].T

    @pl.loop(0, 4)
    def _(k):
        x_ready(k)
        c[k] = tn(x[k], dab[:ROWS, :]).astype(BF)
        dy_ready(k)
        r[k] = nn(hst, dy[k]).astype(BF)
        for copy in stores(place[k], k, c, r, 0):
            copy.start()
        for copy in arrivals(k):
            copy.wait()
        for copy in stores(other_place[k], k, c_in, r_in, 3):
            copy.start()

    @pl.loop(0, 4)
    def _(k):
        for copy in stores(place[k], k, c, r, 0) + stores(other_place[k], k, c_in, r_in, 3):
            copy.wait()


def own_gradients(place, other_place, xs, dys, came, dab, hs, columns, rows, later):
    scratch = PIECES + PIECES[2:] + [pltpu.SemaphoreType.DMA((4,)), pltpu.SemaphoreType.DMA((4, 2))]
    scratch += [pltpu.SemaphoreType.DMA((2, 4)), pltpu.SemaphoreType.DMA((6, 4))]
    outs = [(HBM, sds((8 * COLS, HID)))] * 2 + [(HBM, sds((HID, 8 * COLS))), (VMEM, sds((8, 128), F32))]
    ins = [SMEM] * 2 + [HBM] * 9 + [VMEM] * 2 + [HBM] * 2 + [ANY]
    kernel = call(own_gradient_kernel, ins, outs, scratch, us=12, mib=MOST)
    return kernel(place, other_place, *xs, *dys, came, dab, hs, columns, rows, later)


def total_kernel(expert, *refs):
    terms, out = refs[:3], refs[-1]
    lane = lax.broadcasted_iota(jnp.int32, (128, PAD), 1)
    gates = sum(term[ROWS:, :].astype(F32) for term in terms)
    for i in range(ROWS // 128):
        rows = pl.ds(128 * i, 128)
        out[rows, :COLS] = sum(term[rows, :].astype(F32) for term in terms).astype(BF)
        gate = jnp.broadcast_to(gates[0:1, 128 * i : 128 * i + 128], (128, 128)).T
        high = gate.astype(BF).astype(F32)
        spread = jnp.where(lane == expert[0], high, 0.0) + jnp.where(lane == expert[0] + 64, gate - high, 0.0)
        out[rows, COLS:] = spread.astype(BF)


def total(expert, terms, *later):
    outs = [(VMEM, sds((ROWS, COLS + PAD)))]
    ins = [SMEM] + [VMEM] * 3 + [ANY] * len(later)
    return call(total_kernel, ins, outs)(expert, *terms, *later)[0]


def after(v, *later):
    return pl.pallas_call(
        lambda *refs: None,
        in_specs=[HBM] + [ANY] * len(later),
        out_specs=HBM,
        out_shape=sds(v.shape, v.dtype),
        input_output_aliases={0: 0},
    )(v, *later)


def exchange(v):
    return lax.all_to_all(v.reshape(16, ROOM, -1), ("x", "z"), 0, 0, tiled=True).reshape(ROWS, -1)


def ring(v):
    return [v, meet(v, 0), meet(v, 1)]


def add(*terms):
    return sum(term.astype(F32) for term in terms).astype(BF)


def local(tokens, cotangent, ids, gates, wg, wu, wd):
    core, iy = lax.axis_index("core"), lax.axis_index("y")
    expert = (lax.axis_index("x") * 4 + lax.axis_index("z")).astype(jnp.int32).reshape(1)
    ys = [iy, jnp.where(core == 0, iy ^ 1, 3 - iy), jnp.where(core == 0, 3 - iy, iy ^ 1), (iy + 2) % 4]
    place = jnp.stack([2 * y + core for y in ys]).astype(jnp.int32)
    other_place = jnp.stack([2 * ys[k] + 1 - core for k in (0, 2, 1, 3)]).astype(jnp.int32)
    wg, wu, wd = wg[0], wu[0], wd[0]

    send_x, onehot, weights = dispatch(ids.T, gates.T.astype(F32), tokens)
    rests = ring(cotangent[:, DY_CUT:])
    rests.append(meet(rests[1], 1))
    send_dy = second_dispatch(onehot, weights, cotangent, rests)
    ws = (wg, wu, swap(wg), swap(wu))
    ds = (wd, swap(wd))
    xs = ring(after(exchange(send_x), ws[2], ws[3], ds[1]))
    x_last = meet(xs[1], 1)
    came = exchange(after(send_dy, xs[0]))
    gate = came[:, -PAD:]
    dys = ring(came[:, :DY_CUT])
    dys[1] = after(dys[1], dys[2])
    dy_last = meet(dys[1], 1)

    ws, ds = pack(*ws, *ds)
    first = first_hidden(range(3), place, xs, ws)
    keep, send, raw = middle(place, x_last, dys, came, ws, ds, first)
    s, slope, h = activation(keep, swap(send))
    keep, send = raw_rest(range(3, 4), place, [dy_last], came, ds, raw)
    dab, hs = gradients(keep, swap(send), s, slope, h, gate)
    dab_other, hs_other = swap(dab), swap(hs)

    def part(k, *later):
        return input_part(k, place, dab, dab_other, ws, *later)

    opposite = part(3)
    near = part(2, opposite)
    own = part(1, near)
    opposite, near = meet(opposite, 1), meet(near, 1)
    own = add(own, opposite)
    rest = meet(own, 0)
    xs, dys = xs + [x_last], dys + [dy_last]
    columns, rows = other_gradients(xs, dys, came, dab_other, hs_other, own)
    columns, rows = swap(columns), swap(rows)
    share = total(expert, (part(0, own), near, rest))
    gate_grad, up_grad, down_grad, done = own_gradients(place, other_place, xs, dys, came, dab, hs, columns, rows, share)
    input_grad, slot_grad = combine(exchange(share), onehot, ids, done)
    return input_grad, slot_grad, gate_grad[None], up_grad[None], down_grad[None]


def solution(mesh):
    torus = Mesh(mesh.devices.reshape(4, 4, 4, 2), ("x", "z", "y", "core"))
    ep, etp = ("x", "z"), ("y", "core")
    in_specs = (
        P(ep, etp),
        P(ep, etp),
        P(ep, None),
        P(ep, None),
        P(ep, None, etp),
        P(ep, None, etp),
        P(ep, etp, None),
    )
    out_specs = (P(ep, etp), P(ep, None), P(ep, None, etp), P(ep, None, etp), P(ep, etp, None))
    return jax.shard_map(local, mesh=torus, in_specs=in_specs, out_specs=out_specs, check_vma=False)
```

```python
import functools

import jax
import jax.numpy as jnp
from jax import lax
from jax.experimental import pallas as pl
from jax.experimental.pallas import tpu as pltpu
from jax.sharding import Mesh, PartitionSpec as P

BF, F32 = jnp.bfloat16, jnp.float32
ROWS, COLS, HID, PAD, ROOM, TAIL = 640, 896, 256, 128, 40, 16
SWAP = [(0, 1), (1, 0)]
ANY = pl.BlockSpec(memory_space=pl.ANY)
MOST = 61
DY_CUT = 512
DY_REST = 896 - DY_CUT
OUT_CUT = 640
OUT_REST = 896 - OUT_CUT
RATE = 3e10
VMEM = pl.BlockSpec(memory_space=pltpu.VMEM)
SMEM = pl.BlockSpec(memory_space=pltpu.SMEM)
HBM = pl.BlockSpec(memory_space=pltpu.HBM)


def partner(i, core, step):
    return i ^ 1 if core == step else 3 - i


MEET = tuple(
    [(2 * i + c, 2 * partner(i, c, step) + c) for i in range(4) for c in range(2)] for step in range(2)
)


def meet(v, step):
    return lax.ppermute(v, ("y", "core"), MEET[step])


def swap(v):
    return lax.ppermute(v, "core", SWAP)


def nn(left, right):
    return jnp.dot(left, right, preferred_element_type=F32)


def nt(left, right):
    return lax.dot_general(left, right, (((1,), (1,)), ((), ())), preferred_element_type=F32)


def tn(left, right):
    return lax.dot_general(left, right, (((0,), (0,)), ((), ())), preferred_element_type=F32)


def sds(shape, dtype=BF):
    return jax.ShapeDtypeStruct(shape, dtype)


def call(kernel, ins, outs, scratch=(), us=1, mib=24):
    return pl.pallas_call(
        kernel,
        in_specs=ins,
        out_specs=[spec for spec, _ in outs],
        out_shape=[shape for _, shape in outs],
        scratch_shapes=scratch,
        compiler_params=pltpu.CompilerParams(vmem_limit_bytes=mib * 2**20),
        cost_estimate=pl.CostEstimate(flops=int(us * RATE), bytes_accessed=10000, transcendentals=0),
    )


def dispatch_kernel(ids, gates, x, send_x, onehot, weights):
    expert = lax.broadcasted_iota(jnp.int32, (16, 64), 0)
    named = jnp.zeros((16, 64), F32)
    weight = jnp.zeros((16, 64), F32)
    for k in range(8):
        here = ids[k : k + 1, :] == expert
        named = named + jnp.where(here, 1.0, 0.0)
        weight = weight + jnp.where(here, gates[k : k + 1, :], 0.0)
    one, two = (lax.broadcasted_iota(jnp.int32, (64, 64), axis) for axis in range(2))
    rank = nn(named.astype(BF), jnp.where(one < two, 1.0, 0.0).astype(BF)).astype(jnp.int32)
    slot = lax.broadcasted_iota(jnp.int32, (ROOM, 64), 0)
    picks, sums = [], []
    for e in range(16):
        pick = jnp.where((rank[e : e + 1, :] == slot) & (named[e : e + 1, :] > 0.0), 1.0, 0.0)
        picks.append(pick)
        sums.append(jnp.sum(pick * weight[e : e + 1, :], axis=1, keepdims=True))
    pick = jnp.concatenate(picks, axis=0).astype(BF)
    onehot[...] = pick
    send_x[...] = nn(pick, x[...]).astype(BF)
    weights[...] = jnp.broadcast_to(jnp.concatenate(sums, axis=0), (ROWS, PAD)).astype(BF)


def dispatch(ids, gates, x):
    outs = [(VMEM, sds((ROWS, COLS))), (VMEM, sds((ROWS, 64))), (VMEM, sds((ROWS, PAD)))]
    return call(dispatch_kernel, [VMEM] * 3, outs, us=3)(ids, gates, x)


def second_dispatch_kernel(onehot, weights, dy, *refs):
    rests, out = refs[:2], refs[2]
    pick = onehot[...]
    out[:, :DY_CUT] = nn(pick, dy[:, :DY_CUT]).astype(BF)
    for k in range(4):
        lo = DY_CUT + DY_REST * k
        out[:, lo : lo + DY_REST] = nn(pick, rests[k // 2][64 * (k % 2) : 64 * (k % 2) + 64, :]).astype(BF)
    out[:, -PAD:] = weights[...]


def second_dispatch(onehot, weights, dy, rests):
    outs = [(VMEM, sds((ROWS, DY_CUT + 4 * DY_REST + PAD)))]
    return call(second_dispatch_kernel, [VMEM] * 5, outs, us=3)(onehot, weights, dy, *rests)[0]


def first_combine_kernel(back, onehot, _, *outs):
    pick = onehot[...]
    for k in range(4):
        outs[k // 2][64 * (k % 2) : 64 * (k % 2) + 64, :] = tn(pick, back[:, OUT_REST * k : OUT_REST * k + OUT_REST])


def first_combine(back, onehot, later):
    outs = [(VMEM, sds((128, OUT_REST), F32))] * 2
    return call(first_combine_kernel, [VMEM] * 2 + [ANY], outs, us=2)(back, onehot, later)


def combine_kernel(back, onehot, ids, one, two, *refs):
    grad, gate = refs[-2:]
    pick = onehot[...]
    grad[:, :OUT_CUT] = tn(pick, back[:, :OUT_CUT]).astype(BF)
    grad[:, OUT_CUT:] = (one[...] + two[...]).astype(BF)
    sums = tn(pick, back[:, OUT_CUT:])
    lane = lax.broadcasted_iota(jnp.int32, (64, PAD), 1)
    total = jnp.zeros((64, PAD), F32)
    for k in range(8):
        mine = ids[:, k : k + 1]
        value = jnp.sum(jnp.where((lane == mine) | (lane == mine + 64), sums, 0.0), axis=1, keepdims=True)
        total = total + jnp.where(lane == k, value, 0.0)
    gate[...] = total[:, :8]


def combine(back, onehot, ids, terms, later):
    outs = [(VMEM, sds((64, COLS))), (VMEM, sds((64, 8), F32))]
    return call(combine_kernel, [VMEM] * 5 + [ANY], outs, us=3)(back, onehot, ids, *terms, later)


def block(ref, i):
    return ref.at[pl.ds(pl.multiple_of(i * COLS, COLS), COLS), :]


def column_block(ref, i):
    return ref.at[:, pl.ds(pl.multiple_of(i * COLS, COLS), COLS)]


def pack_kernel(*refs):
    weights, (columns, rows, w, d, sems) = refs[:6], refs[6:]
    loads, stores = [], []
    for j in range(6):
        buffer, out = (w.at[j], columns.at[:, pl.ds(HID * j, HID)]) if j < 4 else (d.at[j - 4], rows.at[pl.ds(HID * (j - 4), HID), :])
        loads.append(pltpu.make_async_copy(weights[j], buffer, sems.at[0, j]))
        stores.append(pltpu.make_async_copy(buffer, out, sems.at[1, j]))
    for copy in loads:
        copy.start()
    for load, store in zip(loads, stores):
        load.wait()
        store.start()
    for copy in stores:
        copy.wait()


def pack(*weights):
    scratch = [pltpu.VMEM((4, 8 * COLS, HID), BF), pltpu.VMEM((2, HID, 8 * COLS), BF), pltpu.SemaphoreType.DMA((2, 6))]
    outs = [(HBM, sds((8 * COLS, 4 * HID))), (HBM, sds((2 * HID, 8 * COLS)))]
    return call(pack_kernel, [HBM] * 6, outs, scratch, us=13, mib=MOST)(*weights)


def hidden_steps(ks, place, xs, ws, x, w, acc, sems):
    def copies(n, src):
        i = place[ks[0] + n]
        first = pltpu.make_async_copy(src, x.at[n], sems.at[1, n])
        return [first, pltpu.make_async_copy(block(ws, i), w.at[n], sems.at[0, n])]

    for n in range(len(ks)):
        for copy in copies(n, xs[n]):
            copy.start()

    @pl.loop(0, len(ks))
    def _(n):
        for copy in copies(n, xs[0]):
            copy.wait()
        acc[...] += nn(x[n], w[n])


def hidden_scratch(n):
    return [pltpu.VMEM((n, ROWS, COLS), BF), pltpu.VMEM((n, COLS, 4 * HID), BF), pltpu.SemaphoreType.DMA((2, n))]


def first_hidden_kernel(ks, place, *refs):
    n = len(ks)
    ws, acc, x, w, sems = refs[n:]
    acc[...] = jnp.zeros_like(acc)
    hidden_steps(ks, place, refs[:n], ws, x, w, acc, sems)


def first_hidden(ks, place, xs, ws):
    outs = [(VMEM, sds((ROWS, 4 * HID), F32))]
    kernel = functools.partial(first_hidden_kernel, ks)
    ins = [SMEM] + [HBM] * (len(ks) + 1)
    return call(kernel, ins, outs, hidden_scratch(len(ks)), us=8, mib=MOST)(place, *xs, ws)[0]


def dy_copies(k, ring_part, came, out, sems):
    rest = came.at[:, pl.ds(pl.multiple_of(DY_CUT + DY_REST * k, 128), DY_REST)]
    return [
        pltpu.make_async_copy(ring_part, out.at[:, pl.ds(0, DY_CUT)], sems.at[0]),
        pltpu.make_async_copy(rest, out.at[:, pl.ds(DY_CUT, DY_REST)], sems.at[1]),
    ]


def raw_steps(ks, place, dys, came, ws, dy, w, acc, sems):
    def copies(n, src):
        i = place[ks[0] + n]
        pieces = dy_copies(ks[0] + n, src, came, dy.at[n], sems.at[n])
        return pieces + [pltpu.make_async_copy(column_block(ws, i), w.at[n], sems.at[n, 2])]

    for n in range(len(ks)):
        for copy in copies(n, dys[n]):
            copy.start()

    @pl.loop(0, len(ks))
    def _(n):
        for copy in copies(n, dys[0]):
            copy.wait()
        acc[...] += nt(dy[n], w[n])


def raw_scratch(n):
    return [pltpu.VMEM((n, ROWS, COLS), BF), pltpu.VMEM((n, 2 * HID, COLS), BF), pltpu.SemaphoreType.DMA((n, 3))]


def middle_kernel(place, x_last, d0, d1, d2, came, *refs):
    ws, ds, first, keep, send, raw, acc, x, w, sems, dy, v, dsems = refs
    acc[...] = first[...]
    hidden_steps(range(3, 4), place, [x_last], ws, x, w, acc, sems)
    keep[...] = acc[:, : 2 * HID]
    send[...] = acc[:, 2 * HID :]
    raw[...] = jnp.zeros_like(raw)
    raw_steps(range(3), place, [d0, d1, d2], came, ds, dy, v, raw, dsems)


def middle(place, x_last, dys, came, ws, ds, first):
    outs = [(VMEM, sds((ROWS, 2 * HID), F32))] * 3
    scratch = [pltpu.VMEM((ROWS, 4 * HID), F32)] + hidden_scratch(1) + raw_scratch(3)
    ins = [SMEM] + [HBM] * 7 + [VMEM]
    return call(middle_kernel, ins, outs, scratch, us=12, mib=MOST)(place, x_last, *dys, came, ws, ds, first)


def activation_kernel(keep, came, s_ref, slope_ref, h_ref):
    for lo in range(0, ROWS, 128):
        rows = pl.ds(lo, 128)
        ab = keep[rows, :] + came[rows, :]
        av, bv = ab[:, :HID], ab[:, HID:]
        sig = jax.nn.sigmoid(av)
        s = av * sig
        s_ref[rows, :] = s
        h_ref[rows, :] = s * bv
        slope_ref[rows, :] = bv * sig * (1.0 + av * (1.0 - sig))


def activation(keep, came):
    return call(activation_kernel, [VMEM] * 2, [(VMEM, sds((ROWS, HID), F32))] * 3)(keep, came)


def raw_kernel(ks, place, *refs):
    n = len(ks)
    came, ws, first, keep, send, acc, dy, w, sems = refs[n:]
    acc[...] = first[...]
    raw_steps(ks, place, refs[:n], came, ws, dy, w, acc, sems)
    keep[...] = acc[:, :HID]
    send[...] = acc[:, HID:]


def raw_rest(ks, place, dys, came, ws, first):
    outs = [(VMEM, sds((ROWS, HID), F32))] * 2
    scratch = [pltpu.VMEM((ROWS, 2 * HID), F32)] + raw_scratch(len(ks))
    ins = [SMEM] + [HBM] * (len(ks) + 2) + [VMEM]
    return call(functools.partial(raw_kernel, ks), ins, outs, scratch, us=3, mib=58)(place, *dys, came, ws, first)


def gradient_kernel(keep, came, s_ref, slope_ref, h_ref, gate, dab, hs):
    sums = []
    for i in range(ROWS // 128):
        rows = pl.ds(128 * i, 128)
        g, raw, h = gate[rows, 0:1].astype(F32), keep[rows, :] + came[rows, :], h_ref[rows, :]
        value = jnp.sum(h * raw, axis=1, keepdims=True)
        sums.append(jnp.broadcast_to(value, (128, 128)).T[0:1, :])
        dh = g * raw
        dab[rows, :HID] = (dh * slope_ref[rows, :]).astype(BF)
        dab[rows, HID:] = (dh * s_ref[rows, :]).astype(BF)
        hs[rows, :] = (g * h).astype(BF)
    tail = [jnp.concatenate(sums[:4], axis=1), jnp.concatenate([sums[4], jnp.zeros((1, 384), F32)], axis=1)]
    dab[ROWS:, :] = jnp.concatenate(tail + [jnp.zeros((TAIL - 2, 512), F32)], axis=0).astype(BF)


def gradients(keep, came, s, slope, h, gate):
    outs = [(VMEM, sds((ROWS + TAIL, 2 * HID))), (VMEM, sds((ROWS, HID)))]
    return call(gradient_kernel, [VMEM] * 6, outs)(keep, came, s, slope, h, gate)


def input_kernel(k, place, own, other, *refs):
    ws, (out, w, grads, sem) = refs[0], refs[-4:]
    start = pl.multiple_of(place[k] * COLS, COLS)
    copy = pltpu.make_async_copy(ws.at[pl.ds(start, OUT_CUT), :], w, sem)
    copy.start()
    grads[:, : 2 * HID], grads[:, 2 * HID :] = own[:ROWS, :], other[:ROWS, :]
    tail = own[ROWS:, :].astype(F32) + other[ROWS:, :].astype(F32)
    row = jnp.concatenate([tail[0:1, :], tail[1:2, :128]], axis=1)
    out[ROWS:, :] = jnp.concatenate([row, jnp.zeros((TAIL - 1, OUT_CUT), F32)], axis=0).astype(BF)
    copy.wait()
    out[:ROWS, :] = nt(grads[...], w[...]).astype(BF)


def input_part(k, place, own, other, ws, *later):
    scratch = [pltpu.VMEM((OUT_CUT, 4 * HID), BF), pltpu.VMEM((ROWS, 4 * HID), BF), pltpu.SemaphoreType.DMA]
    outs = [(VMEM, sds((ROWS + TAIL, OUT_CUT)))]
    ins = [SMEM, VMEM, VMEM, HBM] + [ANY] * len(later)
    return call(functools.partial(input_kernel, k), ins, outs, scratch, us=4, mib=51)(place, own, other, ws, *later)[0]


def rest_kernel(place, own, other, ws, _, out, w, grads, sems):
    copies = []
    for k in range(4):
        start = pl.multiple_of(place[k] * COLS + OUT_CUT, 128)
        copies.append(pltpu.make_async_copy(ws.at[pl.ds(start, OUT_REST), :], w.at[k], sems.at[k]))
    for copy in copies:
        copy.start()
    grads[:, : 2 * HID], grads[:, 2 * HID :] = own[:ROWS, :], other[:ROWS, :]
    for k in range(4):
        copies[k].wait()
        out[:, OUT_REST * k : OUT_REST * k + OUT_REST] = nt(grads[...], w[k]).astype(BF)


def rest_parts(place, own, other, ws, later):
    scratch = [pltpu.VMEM((4, OUT_REST, 4 * HID), BF), pltpu.VMEM((ROWS, 4 * HID), BF), pltpu.SemaphoreType.DMA((4,))]
    outs = [(VMEM, sds((ROWS, 4 * OUT_REST)))]
    return call(rest_kernel, [SMEM, VMEM, VMEM, HBM, ANY], outs, scratch, us=4, mib=51)(place, own, other, ws, later)[0]


def stream(refs, buffer, sems):
    def load(k, src):
        return pltpu.make_async_copy(src, buffer.at[k], sems.at[k])

    for k, ref in enumerate(refs):
        load(k, ref).start()
    return lambda k: load(k, refs[0]).wait()


def dy_stream(refs, came, buffer, sems):
    for k, ref in enumerate(refs):
        for copy in dy_copies(k, ref, came, buffer.at[k], sems.at[k]):
            copy.start()

    def ready(k):
        for copy in dy_copies(k, refs[0], came, buffer.at[k], sems.at[k]):
            copy.wait()

    return ready


def other_gradient_kernel(*refs):
    xs, dys, (came, dab, hs, _, columns, rows, x, dy, c, r, xsems, dsems, sems) = refs[:4], refs[4:8], refs[8:]
    x_ready, dy_ready = stream(xs, x, xsems), dy_stream(dys, came, dy, dsems)

    def stores(k):
        return [
            pltpu.make_async_copy(c.at[k], columns.at[k], sems.at[0, k]),
            pltpu.make_async_copy(r.at[k], rows.at[k], sems.at[1, k]),
        ]

    hst = hs[...].T

    @pl.loop(0, 4)
    def _(k):
        x_ready(k)
        c[k] = tn(x[k], dab[:ROWS, :]).astype(BF)
        dy_ready(k)
        r[k] = nn(hst, dy[k]).astype(BF)
        for copy in stores(k):
            copy.start()

    @pl.loop(0, 4)
    def _(k):
        for copy in stores(k):
            copy.wait()


PIECES = [pltpu.VMEM((4, ROWS, COLS), BF)] * 2 + [pltpu.VMEM((4, COLS, 2 * HID), BF), pltpu.VMEM((4, HID, COLS), BF)]


def other_gradients(xs, dys, came, dab, hs, later):
    scratch = PIECES + [pltpu.SemaphoreType.DMA((4,)), pltpu.SemaphoreType.DMA((4, 2)), pltpu.SemaphoreType.DMA((2, 4))]
    outs = [(HBM, sds((4, COLS, 2 * HID))), (HBM, sds((4, HID, COLS)))]
    ins = [HBM] * 9 + [VMEM] * 2 + [ANY]
    return call(other_gradient_kernel, ins, outs, scratch, us=10, mib=MOST)(*xs, *dys, came, dab, hs, later)


def own_gradient_kernel(place, other_place, *refs):
    xs, dys, came, refs = refs[:4], refs[4:8], refs[8], refs[9:]
    dab, hs, columns, rows, _, g, u, d, token, x, dy, c, r, c_in, r_in, xsems, dsems, isems, sems = refs
    token[...] = jnp.zeros_like(token)
    x_ready, dy_ready = stream(xs, x, xsems), dy_stream(dys, came, dy, dsems)

    def arrivals(k):
        return [
            pltpu.make_async_copy(columns.at[k], c_in.at[k], isems.at[0, k]),
            pltpu.make_async_copy(rows.at[k], r_in.at[k], isems.at[1, k]),
        ]

    def stores(i, k, cols, part, row):
        return [
            pltpu.make_async_copy(cols.at[k, :, pl.ds(0, HID)], block(g, i), sems.at[row, k]),
            pltpu.make_async_copy(cols.at[k, :, pl.ds(HID, HID)], block(u, i), sems.at[row + 1, k]),
            pltpu.make_async_copy(part.at[k], column_block(d, i), sems.at[row + 2, k]),
        ]

    for k in range(4):
        for copy in arrivals(k):
            copy.start()
    hst = hs[...].T

    @pl.loop(0, 4)
    def _(k):
        x_ready(k)
        c[k] = tn(x[k], dab[:ROWS, :]).astype(BF)
        dy_ready(k)
        r[k] = nn(hst, dy[k]).astype(BF)
        for copy in stores(place[k], k, c, r, 0):
            copy.start()
        for copy in arrivals(k):
            copy.wait()
        for copy in stores(other_place[k], k, c_in, r_in, 3):
            copy.start()

    @pl.loop(0, 4)
    def _(k):
        for copy in stores(place[k], k, c, r, 0) + stores(other_place[k], k, c_in, r_in, 3):
            copy.wait()


def own_gradients(place, other_place, xs, dys, came, dab, hs, columns, rows, later):
    scratch = PIECES + PIECES[2:] + [pltpu.SemaphoreType.DMA((4,)), pltpu.SemaphoreType.DMA((4, 2))]
    scratch += [pltpu.SemaphoreType.DMA((2, 4)), pltpu.SemaphoreType.DMA((6, 4))]
    outs = [(HBM, sds((8 * COLS, HID)))] * 2 + [(HBM, sds((HID, 8 * COLS))), (VMEM, sds((8, 128), F32))]
    ins = [SMEM] * 2 + [HBM] * 9 + [VMEM] * 2 + [HBM] * 2 + [ANY]
    kernel = call(own_gradient_kernel, ins, outs, scratch, us=12, mib=MOST)
    return kernel(place, other_place, *xs, *dys, came, dab, hs, columns, rows, later)


def total_kernel(expert, *refs):
    terms, out = refs[:3], refs[-1]
    lane = lax.broadcasted_iota(jnp.int32, (128, PAD), 1)
    gates = sum(term[ROWS:, :].astype(F32) for term in terms)
    for i in range(ROWS // 128):
        rows = pl.ds(128 * i, 128)
        out[rows, :OUT_CUT] = sum(term[rows, :].astype(F32) for term in terms).astype(BF)
        gate = jnp.broadcast_to(gates[0:1, 128 * i : 128 * i + 128], (128, 128)).T
        high = gate.astype(BF).astype(F32)
        spread = jnp.where(lane == expert[0], high, 0.0) + jnp.where(lane == expert[0] + 64, gate - high, 0.0)
        out[rows, OUT_CUT:] = spread.astype(BF)


def total(expert, terms, *later):
    outs = [(VMEM, sds((ROWS, OUT_CUT + PAD)))]
    ins = [SMEM] + [VMEM] * 3 + [ANY] * len(later)
    return call(total_kernel, ins, outs)(expert, *terms, *later)[0]


def after(v, *later):
    return pl.pallas_call(
        lambda *refs: None,
        in_specs=[HBM] + [ANY] * len(later),
        out_specs=HBM,
        out_shape=sds(v.shape, v.dtype),
        input_output_aliases={0: 0},
    )(v, *later)


def exchange(v):
    return lax.all_to_all(v.reshape(16, ROOM, -1), ("x", "z"), 0, 0, tiled=True).reshape(ROWS, -1)


def ring(v):
    return [v, meet(v, 0), meet(v, 1)]


def add(*terms):
    return sum(term.astype(F32) for term in terms).astype(BF)


def local(tokens, cotangent, ids, gates, wg, wu, wd):
    core, iy = lax.axis_index("core"), lax.axis_index("y")
    expert = (lax.axis_index("x") * 4 + lax.axis_index("z")).astype(jnp.int32).reshape(1)
    ys = [iy, jnp.where(core == 0, iy ^ 1, 3 - iy), jnp.where(core == 0, 3 - iy, iy ^ 1), (iy + 2) % 4]
    place = jnp.stack([2 * y + core for y in ys]).astype(jnp.int32)
    other_place = jnp.stack([2 * ys[k] + 1 - core for k in (0, 2, 1, 3)]).astype(jnp.int32)
    wg, wu, wd = wg[0], wu[0], wd[0]

    send_x, onehot, weights = dispatch(ids.T, gates.T.astype(F32), tokens)
    pair = cotangent[:, DY_CUT:]
    pair = jnp.concatenate([pair, meet(pair, 0)])
    rests = [pair, meet(pair, 1)]
    send_dy = second_dispatch(onehot, weights, cotangent, rests)
    ws = (wg, wu, swap(wg), swap(wu))
    ds = (wd, swap(wd))
    xs = ring(after(exchange(send_x), ws[2], ws[3], ds[1]))
    x_last = meet(xs[1], 1)
    came = exchange(after(send_dy, xs[0]))
    gate = came[:, -PAD:]
    dys = ring(came[:, :DY_CUT])
    dys[1] = after(dys[1], dys[2])
    dy_last = meet(dys[1], 1)

    ws, ds = pack(*ws, *ds)
    first = first_hidden(range(3), place, xs, ws)
    keep, send, raw = middle(place, x_last, dys, came, ws, ds, first)
    s, slope, h = activation(keep, swap(send))
    keep, send = raw_rest(range(3, 4), place, [dy_last], came, ds, raw)
    dab, hs = gradients(keep, swap(send), s, slope, h, gate)
    dab_other, hs_other = swap(dab), swap(hs)

    def part(k, *later):
        return input_part(k, place, dab, dab_other, ws, *later)

    opposite = part(3)
    near = part(2, opposite)
    rest_back = exchange(rest_parts(place, dab, dab_other, ws, near))
    own = part(1, near)
    opposite, near = meet(opposite, 1), meet(near, 1)
    own = add(own, opposite)
    rest = meet(own, 0)
    xs, dys = xs + [x_last], dys + [dy_last]
    columns, rows = other_gradients(xs, dys, came, dab_other, hs_other, own)
    columns, rows = swap(columns), swap(rows)
    share = total(expert, (part(0, own), near, rest))
    gate_grad, up_grad, down_grad, done = own_gradients(place, other_place, xs, dys, came, dab, hs, columns, rows, share)
    ends = first_combine(rest_back, onehot, share)
    ends = ends[0] + meet(ends[1], 1)
    ends = (ends[:64], meet(ends[64:], 0))
    input_grad, slot_grad = combine(exchange(share), onehot, ids, ends, done)
    return input_grad, slot_grad, gate_grad[None], up_grad[None], down_grad[None]


def solution(mesh):
    torus = Mesh(mesh.devices.reshape(4, 4, 4, 2), ("x", "z", "y", "core"))
    ep, etp = ("x", "z"), ("y", "core")
    in_specs = (
        P(ep, etp),
        P(ep, etp),
        P(ep, None),
        P(ep, None),
        P(ep, None, etp),
        P(ep, None, etp),
        P(ep, etp, None),
    )
    out_specs = (P(ep, etp), P(ep, None), P(ep, None, etp), P(ep, None, etp), P(ep, etp, None))
    return jax.shard_map(local, mesh=torus, in_specs=in_specs, out_specs=out_specs, check_vma=False)
```

```python
import functools

import jax
import jax.numpy as jnp
from jax import lax
from jax.experimental import pallas as pl
from jax.experimental.pallas import tpu as pltpu
from jax.sharding import Mesh, PartitionSpec as P

BF, F32 = jnp.bfloat16, jnp.float32
ROWS, COLS, HID, PAD, ROOM, TAIL = 640, 896, 256, 128, 40, 16
SWAP = [(0, 1), (1, 0)]
ANY = pl.BlockSpec(memory_space=pl.ANY)
MOST = 61
DY_CUT = 512
DY_REST = 896 - DY_CUT
OUT_CUT = 640
OUT_REST = 896 - OUT_CUT
RATE = 3e10
VMEM = pl.BlockSpec(memory_space=pltpu.VMEM)
SMEM = pl.BlockSpec(memory_space=pltpu.SMEM)
HBM = pl.BlockSpec(memory_space=pltpu.HBM)


def partner(i, core, step):
    return i ^ 1 if core == step else 3 - i


MEET = tuple(
    [(2 * i + c, 2 * partner(i, c, step) + c) for i in range(4) for c in range(2)] for step in range(2)
)


def meet(v, step):
    return lax.ppermute(v, ("y", "core"), MEET[step])


def swap(v):
    return lax.ppermute(v, "core", SWAP)


def nn(left, right):
    return jnp.dot(left, right, preferred_element_type=F32)


def nt(left, right):
    return lax.dot_general(left, right, (((1,), (1,)), ((), ())), preferred_element_type=F32)


def tn(left, right):
    return lax.dot_general(left, right, (((0,), (0,)), ((), ())), preferred_element_type=F32)


def sds(shape, dtype=BF):
    return jax.ShapeDtypeStruct(shape, dtype)


def call(kernel, ins, outs, scratch=(), us=1, mib=24):
    return pl.pallas_call(
        kernel,
        in_specs=ins,
        out_specs=[spec for spec, _ in outs],
        out_shape=[shape for _, shape in outs],
        scratch_shapes=scratch,
        compiler_params=pltpu.CompilerParams(vmem_limit_bytes=mib * 2**20),
        cost_estimate=pl.CostEstimate(flops=int(us * RATE), bytes_accessed=10000, transcendentals=0),
    )


def dispatch_kernel(ids, gates, x, send_x, onehot, weights):
    expert = lax.broadcasted_iota(jnp.int32, (16, 64), 0)
    named = jnp.zeros((16, 64), F32)
    weight = jnp.zeros((16, 64), F32)
    for k in range(8):
        here = ids[k : k + 1, :] == expert
        named = named + jnp.where(here, 1.0, 0.0)
        weight = weight + jnp.where(here, gates[k : k + 1, :], 0.0)
    one, two = (lax.broadcasted_iota(jnp.int32, (64, 64), axis) for axis in range(2))
    rank = nn(named.astype(BF), jnp.where(one < two, 1.0, 0.0).astype(BF)).astype(jnp.int32)
    slot = lax.broadcasted_iota(jnp.int32, (ROOM, 64), 0)
    picks, sums = [], []
    for e in range(16):
        pick = jnp.where((rank[e : e + 1, :] == slot) & (named[e : e + 1, :] > 0.0), 1.0, 0.0)
        picks.append(pick)
        sums.append(jnp.sum(pick * weight[e : e + 1, :], axis=1, keepdims=True))
    pick = jnp.concatenate(picks, axis=0).astype(BF)
    onehot[...] = pick
    send_x[...] = nn(pick, x[...]).astype(BF)
    weights[...] = jnp.broadcast_to(jnp.concatenate(sums, axis=0), (ROWS, PAD)).astype(BF)


def dispatch(ids, gates, x):
    outs = [(VMEM, sds((ROWS, COLS))), (VMEM, sds((ROWS, 64))), (VMEM, sds((ROWS, PAD)))]
    return call(dispatch_kernel, [VMEM] * 3, outs, us=3)(ids, gates, x)


def second_dispatch_kernel(onehot, weights, dy, *refs):
    rests, out = refs[:2], refs[2]
    pick = onehot[...]
    out[:, :DY_CUT] = nn(pick, dy[:, :DY_CUT]).astype(BF)
    for k in range(4):
        lo = DY_CUT + DY_REST * k
        out[:, lo : lo + DY_REST] = nn(pick, rests[k // 2][64 * (k % 2) : 64 * (k % 2) + 64, :]).astype(BF)
    out[:, -PAD:] = weights[...]


def second_dispatch(onehot, weights, dy, rests):
    outs = [(VMEM, sds((ROWS, DY_CUT + 4 * DY_REST + PAD)))]
    return call(second_dispatch_kernel, [VMEM] * 5, outs, us=3)(onehot, weights, dy, *rests)[0]


def first_combine_kernel(back, onehot, _, *outs):
    pick = onehot[...]
    for k in range(4):
        outs[k // 2][64 * (k % 2) : 64 * (k % 2) + 64, :] = tn(pick, back[:, OUT_REST * k : OUT_REST * k + OUT_REST])


def first_combine(back, onehot, later):
    outs = [(VMEM, sds((128, OUT_REST), F32))] * 2
    return call(first_combine_kernel, [VMEM] * 2 + [ANY], outs, us=2)(back, onehot, later)


def combine_kernel(back, onehot, ids, one, two, *refs):
    grad, gate = refs[-2:]
    pick = onehot[...]
    grad[:, :OUT_CUT] = tn(pick, back[:, :OUT_CUT]).astype(BF)
    grad[:, OUT_CUT:] = (one[...] + two[...]).astype(BF)
    sums = tn(pick, back[:, OUT_CUT:])
    lane = lax.broadcasted_iota(jnp.int32, (64, PAD), 1)
    total = jnp.zeros((64, PAD), F32)
    for k in range(8):
        mine = ids[:, k : k + 1]
        value = jnp.sum(jnp.where((lane == mine) | (lane == mine + 64), sums, 0.0), axis=1, keepdims=True)
        total = total + jnp.where(lane == k, value, 0.0)
    gate[...] = total[:, :8]


def combine(back, onehot, ids, terms, later):
    outs = [(VMEM, sds((64, COLS))), (VMEM, sds((64, 8), F32))]
    return call(combine_kernel, [VMEM] * 5 + [ANY], outs, us=3)(back, onehot, ids, *terms, later)


def block(ref, i):
    return ref.at[pl.ds(pl.multiple_of(i * COLS, COLS), COLS), :]


def column_block(ref, i):
    return ref.at[:, pl.ds(pl.multiple_of(i * COLS, COLS), COLS)]


def pack_kernel(*refs):
    weights, (columns, rows, w, d, sems) = refs[:6], refs[6:]
    loads, stores = [], []
    for j in range(6):
        buffer, out = (w.at[j], columns.at[:, pl.ds(HID * j, HID)]) if j < 4 else (d.at[j - 4], rows.at[pl.ds(HID * (j - 4), HID), :])
        loads.append(pltpu.make_async_copy(weights[j], buffer, sems.at[0, j]))
        stores.append(pltpu.make_async_copy(buffer, out, sems.at[1, j]))
    for copy in loads:
        copy.start()
    for load, store in zip(loads, stores):
        load.wait()
        store.start()
    for copy in stores:
        copy.wait()


def pack(*weights):
    scratch = [pltpu.VMEM((4, 8 * COLS, HID), BF), pltpu.VMEM((2, HID, 8 * COLS), BF), pltpu.SemaphoreType.DMA((2, 6))]
    outs = [(HBM, sds((8 * COLS, 4 * HID))), (HBM, sds((2 * HID, 8 * COLS)))]
    return call(pack_kernel, [HBM] * 6, outs, scratch, us=13, mib=MOST)(*weights)


def hidden_steps(ks, place, xs, ws, x, w, acc, sems):
    def copies(n, src):
        i = place[ks[0] + n]
        first = pltpu.make_async_copy(src, x.at[n], sems.at[1, n])
        return [first, pltpu.make_async_copy(block(ws, i), w.at[n], sems.at[0, n])]

    for n in range(len(ks)):
        for copy in copies(n, xs[n]):
            copy.start()

    @pl.loop(0, len(ks))
    def _(n):
        for copy in copies(n, xs[0]):
            copy.wait()
        acc[...] += nn(x[n], w[n])


def hidden_scratch(n):
    return [pltpu.VMEM((n, ROWS, COLS), BF), pltpu.VMEM((n, COLS, 4 * HID), BF), pltpu.SemaphoreType.DMA((2, n))]


def first_hidden_kernel(ks, place, *refs):
    n = len(ks)
    ws, acc, x, w, sems = refs[n:]
    acc[...] = jnp.zeros_like(acc)
    hidden_steps(ks, place, refs[:n], ws, x, w, acc, sems)


def first_hidden(ks, place, xs, ws):
    outs = [(VMEM, sds((ROWS, 4 * HID), F32))]
    kernel = functools.partial(first_hidden_kernel, ks)
    ins = [SMEM] + [HBM] * (len(ks) + 1)
    return call(kernel, ins, outs, hidden_scratch(len(ks)), us=8, mib=MOST)(place, *xs, ws)[0]


def dy_copies(k, ring_part, came, out, sems):
    rest = came.at[:, pl.ds(pl.multiple_of(DY_CUT + DY_REST * k, 128), DY_REST)]
    return [
        pltpu.make_async_copy(ring_part, out.at[:, pl.ds(0, DY_CUT)], sems.at[0]),
        pltpu.make_async_copy(rest, out.at[:, pl.ds(DY_CUT, DY_REST)], sems.at[1]),
    ]


def raw_steps(ks, place, dys, came, ws, dy, w, acc, sems):
    def copies(n, src):
        i = place[ks[0] + n]
        pieces = dy_copies(ks[0] + n, src, came, dy.at[n], sems.at[n])
        return pieces + [pltpu.make_async_copy(column_block(ws, i), w.at[n], sems.at[n, 2])]

    for n in range(len(ks)):
        for copy in copies(n, dys[n]):
            copy.start()

    @pl.loop(0, len(ks))
    def _(n):
        for copy in copies(n, dys[0]):
            copy.wait()
        acc[...] += nt(dy[n], w[n])


def raw_scratch(n):
    return [pltpu.VMEM((n, ROWS, COLS), BF), pltpu.VMEM((n, 2 * HID, COLS), BF), pltpu.SemaphoreType.DMA((n, 3))]


def middle_kernel(place, x_last, d0, d1, d2, came, *refs):
    ws, ds, first, keep, send, raw, acc, x, w, sems, dy, v, dsems = refs
    acc[...] = first[...]
    hidden_steps(range(3, 4), place, [x_last], ws, x, w, acc, sems)
    keep[...] = acc[:, : 2 * HID]
    send[...] = acc[:, 2 * HID :]
    raw[...] = jnp.zeros_like(raw)
    raw_steps(range(3), place, [d0, d1, d2], came, ds, dy, v, raw, dsems)


def middle(place, x_last, dys, came, ws, ds, first):
    outs = [(VMEM, sds((ROWS, 2 * HID), F32))] * 3
    scratch = [pltpu.VMEM((ROWS, 4 * HID), F32)] + hidden_scratch(1) + raw_scratch(3)
    ins = [SMEM] + [HBM] * 7 + [VMEM]
    return call(middle_kernel, ins, outs, scratch, us=12, mib=MOST)(place, x_last, *dys, came, ws, ds, first)


def activation_kernel(keep, came, s_ref, slope_ref, h_ref):
    for lo in range(0, ROWS, 128):
        rows = pl.ds(lo, 128)
        ab = keep[rows, :] + came[rows, :]
        av, bv = ab[:, :HID], ab[:, HID:]
        sig = jax.nn.sigmoid(av)
        s = av * sig
        s_ref[rows, :] = s
        h_ref[rows, :] = s * bv
        slope_ref[rows, :] = bv * sig * (1.0 + av * (1.0 - sig))


def activation(keep, came):
    return call(activation_kernel, [VMEM] * 2, [(VMEM, sds((ROWS, HID), F32))] * 3)(keep, came)


def raw_kernel(ks, place, *refs):
    n = len(ks)
    came, ws, first, keep, send, acc, dy, w, sems = refs[n:]
    acc[...] = first[...]
    raw_steps(ks, place, refs[:n], came, ws, dy, w, acc, sems)
    keep[...] = acc[:, :HID]
    send[...] = acc[:, HID:]


def raw_rest(ks, place, dys, came, ws, first):
    outs = [(VMEM, sds((ROWS, HID), F32))] * 2
    scratch = [pltpu.VMEM((ROWS, 2 * HID), F32)] + raw_scratch(len(ks))
    ins = [SMEM] + [HBM] * (len(ks) + 2) + [VMEM]
    return call(functools.partial(raw_kernel, ks), ins, outs, scratch, us=3, mib=58)(place, *dys, came, ws, first)


def gradient_kernel(keep, came, s_ref, slope_ref, h_ref, gate, dab, hs):
    sums = []
    for i in range(ROWS // 128):
        rows = pl.ds(128 * i, 128)
        g, raw, h = gate[rows, 0:1].astype(F32), keep[rows, :] + came[rows, :], h_ref[rows, :]
        value = jnp.sum(h * raw, axis=1, keepdims=True)
        sums.append(jnp.broadcast_to(value, (128, 128)).T[0:1, :])
        dh = g * raw
        dab[rows, :HID] = (dh * slope_ref[rows, :]).astype(BF)
        dab[rows, HID:] = (dh * s_ref[rows, :]).astype(BF)
        hs[rows, :] = (g * h).astype(BF)
    tail = [jnp.concatenate(sums[:4], axis=1), jnp.concatenate([sums[4], jnp.zeros((1, 384), F32)], axis=1)]
    dab[ROWS:, :] = jnp.concatenate(tail + [jnp.zeros((TAIL - 2, 512), F32)], axis=0).astype(BF)


def gradients(keep, came, s, slope, h, gate):
    outs = [(VMEM, sds((ROWS + TAIL, 2 * HID))), (VMEM, sds((ROWS, HID)))]
    return call(gradient_kernel, [VMEM] * 6, outs)(keep, came, s, slope, h, gate)


def input_kernel(k, place, own, other, *refs):
    ws, (out, w, grads, sem) = refs[0], refs[-4:]
    start = pl.multiple_of(place[k] * COLS, COLS)
    copy = pltpu.make_async_copy(ws.at[pl.ds(start, OUT_CUT), :], w, sem)
    copy.start()
    grads[:, : 2 * HID], grads[:, 2 * HID :] = own[:ROWS, :], other[:ROWS, :]
    tail = own[ROWS:, :].astype(F32) + other[ROWS:, :].astype(F32)
    row = jnp.concatenate([tail[0:1, :], tail[1:2, :128]], axis=1)
    out[ROWS:, :] = jnp.concatenate([row, jnp.zeros((TAIL - 1, OUT_CUT), F32)], axis=0).astype(BF)
    copy.wait()
    out[:ROWS, :] = nt(grads[...], w[...]).astype(BF)


def input_part(k, place, own, other, ws, *later):
    scratch = [pltpu.VMEM((OUT_CUT, 4 * HID), BF), pltpu.VMEM((ROWS, 4 * HID), BF), pltpu.SemaphoreType.DMA]
    outs = [(VMEM, sds((ROWS + TAIL, OUT_CUT)))]
    ins = [SMEM, VMEM, VMEM, HBM] + [ANY] * len(later)
    return call(functools.partial(input_kernel, k), ins, outs, scratch, us=4, mib=51)(place, own, other, ws, *later)[0]


def rest_kernel(place, own, other, ws, _, out, w, grads, sems):
    copies = []
    for k in range(4):
        start = pl.multiple_of(place[k] * COLS + OUT_CUT, 128)
        copies.append(pltpu.make_async_copy(ws.at[pl.ds(start, OUT_REST), :], w.at[k], sems.at[k]))
    for copy in copies:
        copy.start()
    grads[:, : 2 * HID], grads[:, 2 * HID :] = own[:ROWS, :], other[:ROWS, :]
    for k in range(4):
        copies[k].wait()
        out[:, OUT_REST * k : OUT_REST * k + OUT_REST] = nt(grads[...], w[k]).astype(BF)


def rest_parts(place, own, other, ws, later):
    scratch = [pltpu.VMEM((4, OUT_REST, 4 * HID), BF), pltpu.VMEM((ROWS, 4 * HID), BF), pltpu.SemaphoreType.DMA((4,))]
    outs = [(VMEM, sds((ROWS, 4 * OUT_REST)))]
    return call(rest_kernel, [SMEM, VMEM, VMEM, HBM, ANY], outs, scratch, us=4, mib=51)(place, own, other, ws, later)[0]


def stream(refs, buffer, sems):
    def load(k, src):
        return pltpu.make_async_copy(src, buffer.at[k], sems.at[k])

    for k, ref in enumerate(refs):
        load(k, ref).start()
    return lambda k: load(k, refs[0]).wait()


def dy_stream(refs, came, buffer, sems):
    for k, ref in enumerate(refs):
        for copy in dy_copies(k, ref, came, buffer.at[k], sems.at[k]):
            copy.start()

    def ready(k):
        for copy in dy_copies(k, refs[0], came, buffer.at[k], sems.at[k]):
            copy.wait()

    return ready


def other_gradient_kernel(*refs):
    xs, dys, (came, dab, hs, _, columns, rows, x, dy, c, r, xsems, dsems, sems) = refs[:4], refs[4:8], refs[8:]
    x_ready, dy_ready = stream(xs, x, xsems), dy_stream(dys, came, dy, dsems)

    def stores(k):
        return [
            pltpu.make_async_copy(c.at[k], columns.at[k], sems.at[0, k]),
            pltpu.make_async_copy(r.at[k], rows.at[k], sems.at[1, k]),
        ]

    hst = hs[...].T

    @pl.loop(0, 4)
    def _(k):
        x_ready(k)
        c[k] = tn(x[k], dab[:ROWS, :]).astype(BF)
        dy_ready(k)
        r[k] = nn(hst, dy[k]).astype(BF)
        for copy in stores(k):
            copy.start()

    @pl.loop(0, 4)
    def _(k):
        for copy in stores(k):
            copy.wait()


PIECES = [pltpu.VMEM((4, ROWS, COLS), BF)] * 2 + [pltpu.VMEM((4, COLS, 2 * HID), BF), pltpu.VMEM((4, HID, COLS), BF)]


def other_gradients(xs, dys, came, dab, hs, later):
    scratch = PIECES + [pltpu.SemaphoreType.DMA((4,)), pltpu.SemaphoreType.DMA((4, 2)), pltpu.SemaphoreType.DMA((2, 4))]
    outs = [(HBM, sds((4, COLS, 2 * HID))), (HBM, sds((4, HID, COLS)))]
    ins = [HBM] * 9 + [VMEM] * 2 + [ANY]
    return call(other_gradient_kernel, ins, outs, scratch, us=10, mib=MOST)(*xs, *dys, came, dab, hs, later)


def own_gradient_kernel(place, other_place, *refs):
    xs, dys, came, refs = refs[:4], refs[4:8], refs[8], refs[9:]
    dab, hs, columns, rows, _, g, u, d, token, x, dy, c, r, c_in, r_in, xsems, dsems, isems, sems = refs
    token[...] = jnp.zeros_like(token)
    x_ready, dy_ready = stream(xs, x, xsems), dy_stream(dys, came, dy, dsems)

    def arrivals(k):
        return [
            pltpu.make_async_copy(columns.at[k], c_in.at[k], isems.at[0, k]),
            pltpu.make_async_copy(rows.at[k], r_in.at[k], isems.at[1, k]),
        ]

    def stores(i, k, cols, part, row):
        return [
            pltpu.make_async_copy(cols.at[k, :, pl.ds(0, HID)], block(g, i), sems.at[row, k]),
            pltpu.make_async_copy(cols.at[k, :, pl.ds(HID, HID)], block(u, i), sems.at[row + 1, k]),
            pltpu.make_async_copy(part.at[k], column_block(d, i), sems.at[row + 2, k]),
        ]

    for k in range(4):
        for copy in arrivals(k):
            copy.start()
    hst = hs[...].T

    @pl.loop(0, 4)
    def _(k):
        x_ready(k)
        c[k] = tn(x[k], dab[:ROWS, :]).astype(BF)
        dy_ready(k)
        r[k] = nn(hst, dy[k]).astype(BF)
        for copy in stores(place[k], k, c, r, 0):
            copy.start()
        for copy in arrivals(k):
            copy.wait()
        for copy in stores(other_place[k], k, c_in, r_in, 3):
            copy.start()

    @pl.loop(0, 4)
    def _(k):
        for copy in stores(place[k], k, c, r, 0) + stores(other_place[k], k, c_in, r_in, 3):
            copy.wait()


def own_gradients(place, other_place, xs, dys, came, dab, hs, columns, rows, later):
    scratch = PIECES + PIECES[2:] + [pltpu.SemaphoreType.DMA((4,)), pltpu.SemaphoreType.DMA((4, 2))]
    scratch += [pltpu.SemaphoreType.DMA((2, 4)), pltpu.SemaphoreType.DMA((6, 4))]
    outs = [(HBM, sds((8 * COLS, HID)))] * 2 + [(HBM, sds((HID, 8 * COLS))), (VMEM, sds((8, 128), F32))]
    ins = [SMEM] * 2 + [HBM] * 9 + [VMEM] * 2 + [HBM] * 2 + [ANY]
    kernel = call(own_gradient_kernel, ins, outs, scratch, us=1, mib=MOST)
    return kernel(place, other_place, *xs, *dys, came, dab, hs, columns, rows, later)


def total_kernel(expert, *refs):
    terms, out = refs[:3], refs[-1]
    lane = lax.broadcasted_iota(jnp.int32, (128, PAD), 1)
    gates = sum(term[ROWS:, :].astype(F32) for term in terms)
    for i in range(ROWS // 128):
        rows = pl.ds(128 * i, 128)
        out[rows, :OUT_CUT] = sum(term[rows, :].astype(F32) for term in terms).astype(BF)
        gate = jnp.broadcast_to(gates[0:1, 128 * i : 128 * i + 128], (128, 128)).T
        high = gate.astype(BF).astype(F32)
        spread = jnp.where(lane == expert[0], high, 0.0) + jnp.where(lane == expert[0] + 64, gate - high, 0.0)
        out[rows, OUT_CUT:] = spread.astype(BF)


def total(expert, terms, *later):
    outs = [(VMEM, sds((ROWS, OUT_CUT + PAD)))]
    ins = [SMEM] + [VMEM] * 3 + [ANY] * len(later)
    return call(total_kernel, ins, outs)(expert, *terms, *later)[0]


def after(v, *later):
    return pl.pallas_call(
        lambda *refs: None,
        in_specs=[HBM] + [ANY] * len(later),
        out_specs=HBM,
        out_shape=sds(v.shape, v.dtype),
        input_output_aliases={0: 0},
    )(v, *later)


def exchange(v):
    return lax.all_to_all(v.reshape(16, ROOM, -1), ("x", "z"), 0, 0, tiled=True).reshape(ROWS, -1)


def ring(v):
    return [v, meet(v, 0), meet(v, 1)]


def add(*terms):
    return sum(term.astype(F32) for term in terms).astype(BF)


def local(tokens, cotangent, ids, gates, wg, wu, wd):
    core, iy = lax.axis_index("core"), lax.axis_index("y")
    expert = (lax.axis_index("x") * 4 + lax.axis_index("z")).astype(jnp.int32).reshape(1)
    ys = [iy, jnp.where(core == 0, iy ^ 1, 3 - iy), jnp.where(core == 0, 3 - iy, iy ^ 1), (iy + 2) % 4]
    place = jnp.stack([2 * y + core for y in ys]).astype(jnp.int32)
    other_place = jnp.stack([2 * ys[k] + 1 - core for k in (0, 2, 1, 3)]).astype(jnp.int32)
    wg, wu, wd = wg[0], wu[0], wd[0]

    send_x, onehot, weights = dispatch(ids.T, gates.T.astype(F32), tokens)
    pair = cotangent[:, DY_CUT:]
    pair = jnp.concatenate([pair, meet(pair, 0)])
    rests = [pair, meet(pair, 1)]
    send_dy = second_dispatch(onehot, weights, cotangent, rests)
    ws = (wg, wu, swap(wg), swap(wu))
    ds = (wd, swap(wd))
    xs = ring(after(exchange(send_x), ws[2], ws[3], ds[1]))
    x_last = meet(xs[1], 1)
    came = exchange(after(send_dy, xs[0]))
    gate = came[:, -PAD:]
    dys = ring(came[:, :DY_CUT])
    dys[1] = after(dys[1], dys[2])
    dy_last = meet(dys[1], 1)

    ws, ds = pack(*ws, *ds)
    first = first_hidden(range(3), place, xs, ws)
    keep, send, raw = middle(place, x_last, dys, came, ws, ds, first)
    s, slope, h = activation(keep, swap(send))
    keep, send = raw_rest(range(3, 4), place, [dy_last], came, ds, raw)
    dab, hs = gradients(keep, swap(send), s, slope, h, gate)
    dab_other, hs_other = swap(dab), swap(hs)

    def part(k, *later):
        return input_part(k, place, dab, dab_other, ws, *later)

    opposite = part(3)
    near = part(2, opposite)
    rest_back = exchange(rest_parts(place, dab, dab_other, ws, near))
    own = part(1, near)
    opposite, near = meet(opposite, 1), meet(near, 1)
    own = add(own, opposite)
    rest = meet(own, 0)
    xs, dys = xs + [x_last], dys + [dy_last]
    columns, rows = other_gradients(xs, dys, came, dab_other, hs_other, own)
    columns, rows = swap(columns), swap(rows)
    share = total(expert, (part(0, own), near, rest))
    gate_grad, up_grad, down_grad, done = own_gradients(place, other_place, xs, dys, came, dab, hs, columns, rows, share)
    ends = first_combine(rest_back, onehot, share)
    ends = ends[0] + meet(ends[1], 1)
    ends = (ends[:64], meet(ends[64:], 0))
    input_grad, slot_grad = combine(exchange(share), onehot, ids, ends, done)
    return input_grad, slot_grad, gate_grad[None], up_grad[None], down_grad[None]


def solution(mesh):
    torus = Mesh(mesh.devices.reshape(4, 4, 4, 2), ("x", "z", "y", "core"))
    ep, etp = ("x", "z"), ("y", "core")
    in_specs = (
        P(ep, etp),
        P(ep, etp),
        P(ep, None),
        P(ep, None),
        P(ep, None, etp),
        P(ep, None, etp),
        P(ep, etp, None),
    )
    out_specs = (P(ep, etp), P(ep, None), P(ep, None, etp), P(ep, None, etp), P(ep, etp, None))
    return jax.shard_map(local, mesh=torus, in_specs=in_specs, out_specs=out_specs, check_vma=False)
```

```python
import functools

import jax
import jax.numpy as jnp
from jax import lax
from jax.experimental import pallas as pl
from jax.experimental.pallas import tpu as pltpu
from jax.sharding import Mesh, PartitionSpec as P

BF, F32 = jnp.bfloat16, jnp.float32
ROWS, COLS, HID, PAD, ROOM, TAIL = 640, 896, 256, 128, 40, 16
SWAP = [(0, 1), (1, 0)]
ANY = pl.BlockSpec(memory_space=pl.ANY)
MOST = 61
DY_CUT = 512
DY_REST = 896 - DY_CUT
OUT_CUT = 640
OUT_REST = 896 - OUT_CUT
RATE = 3e10
VMEM = pl.BlockSpec(memory_space=pltpu.VMEM)
SMEM = pl.BlockSpec(memory_space=pltpu.SMEM)
HBM = pl.BlockSpec(memory_space=pltpu.HBM)


def partner(i, core, step):
    return i ^ 1 if core == step else 3 - i


MEET = tuple(
    [(2 * i + c, 2 * partner(i, c, step) + c) for i in range(4) for c in range(2)] for step in range(2)
)


def meet(v, step):
    return lax.ppermute(v, ("y", "core"), MEET[step])


def swap(v):
    return lax.ppermute(v, "core", SWAP)


def nn(left, right):
    return jnp.dot(left, right, preferred_element_type=F32)


def nt(left, right):
    return lax.dot_general(left, right, (((1,), (1,)), ((), ())), preferred_element_type=F32)


def tn(left, right):
    return lax.dot_general(left, right, (((0,), (0,)), ((), ())), preferred_element_type=F32)


def sds(shape, dtype=BF):
    return jax.ShapeDtypeStruct(shape, dtype)


def call(kernel, ins, outs, scratch=(), us=1, mib=24):
    return pl.pallas_call(
        kernel,
        in_specs=ins,
        out_specs=[spec for spec, _ in outs],
        out_shape=[shape for _, shape in outs],
        scratch_shapes=scratch,
        compiler_params=pltpu.CompilerParams(vmem_limit_bytes=mib * 2**20),
        cost_estimate=pl.CostEstimate(flops=int(us * RATE), bytes_accessed=10000, transcendentals=0),
    )


def dispatch_kernel(ids, gates, x, send_x, onehot, weights):
    expert = lax.broadcasted_iota(jnp.int32, (16, 64), 0)
    named = jnp.zeros((16, 64), F32)
    weight = jnp.zeros((16, 64), F32)
    for k in range(8):
        here = ids[k : k + 1, :] == expert
        named = named + jnp.where(here, 1.0, 0.0)
        weight = weight + jnp.where(here, gates[k : k + 1, :], 0.0)
    one, two = (lax.broadcasted_iota(jnp.int32, (64, 64), axis) for axis in range(2))
    rank = nn(named.astype(BF), jnp.where(one < two, 1.0, 0.0).astype(BF)).astype(jnp.int32)
    slot = lax.broadcasted_iota(jnp.int32, (ROOM, 64), 0)
    picks, sums = [], []
    for e in range(16):
        pick = jnp.where((rank[e : e + 1, :] == slot) & (named[e : e + 1, :] > 0.0), 1.0, 0.0)
        picks.append(pick)
        sums.append(jnp.sum(pick * weight[e : e + 1, :], axis=1, keepdims=True))
    pick = jnp.concatenate(picks, axis=0).astype(BF)
    onehot[...] = pick
    send_x[...] = nn(pick, x[...]).astype(BF)
    weights[...] = jnp.broadcast_to(jnp.concatenate(sums, axis=0), (ROWS, PAD)).astype(BF)


def dispatch(ids, gates, x):
    outs = [(VMEM, sds((ROWS, COLS))), (VMEM, sds((ROWS, 64))), (VMEM, sds((ROWS, PAD)))]
    return call(dispatch_kernel, [VMEM] * 3, outs, us=3)(ids, gates, x)


def second_dispatch_kernel(onehot, weights, dy, *refs):
    rests, out = refs[:2], refs[2]
    pick = onehot[...]
    out[:, :DY_CUT] = nn(pick, dy[:, :DY_CUT]).astype(BF)
    for k in range(4):
        lo = DY_CUT + DY_REST * k
        out[:, lo : lo + DY_REST] = nn(pick, rests[k // 2][64 * (k % 2) : 64 * (k % 2) + 64, :]).astype(BF)
    out[:, -PAD:] = weights[...]


def second_dispatch(onehot, weights, dy, rests):
    outs = [(VMEM, sds((ROWS, DY_CUT + 4 * DY_REST + PAD)))]
    return call(second_dispatch_kernel, [VMEM] * 5, outs, us=3)(onehot, weights, dy, *rests)[0]


def first_combine_kernel(back, onehot, _, *outs):
    pick = onehot[...]
    for k in range(4):
        outs[k // 2][64 * (k % 2) : 64 * (k % 2) + 64, :] = tn(pick, back[:, OUT_REST * k : OUT_REST * k + OUT_REST])


def first_combine(back, onehot, later):
    outs = [(VMEM, sds((128, OUT_REST), F32))] * 2
    return call(first_combine_kernel, [VMEM] * 2 + [ANY], outs, us=2)(back, onehot, later)


def combine_kernel(back, onehot, ids, one, two, *refs):
    grad, gate = refs[-2:]
    pick = onehot[...]
    grad[:, :OUT_CUT] = tn(pick, back[:, :OUT_CUT]).astype(BF)
    grad[:, OUT_CUT:] = (one[...] + two[...]).astype(BF)
    sums = tn(pick, back[:, OUT_CUT:])
    lane = lax.broadcasted_iota(jnp.int32, (64, PAD), 1)
    total = jnp.zeros((64, PAD), F32)
    for k in range(8):
        mine = ids[:, k : k + 1]
        value = jnp.sum(jnp.where((lane == mine) | (lane == mine + 64), sums, 0.0), axis=1, keepdims=True)
        total = total + jnp.where(lane == k, value, 0.0)
    gate[...] = total[:, :8]


def combine(back, onehot, ids, terms, later):
    outs = [(VMEM, sds((64, COLS))), (VMEM, sds((64, 8), F32))]
    return call(combine_kernel, [VMEM] * 6, outs, us=3)(back, onehot, ids, *terms, later)


def block(ref, i):
    return ref.at[pl.ds(pl.multiple_of(i * COLS, COLS), COLS), :]


def column_block(ref, i):
    return ref.at[:, pl.ds(pl.multiple_of(i * COLS, COLS), COLS)]


def pack_kernel(*refs):
    weights, (columns, rows, w, d, sems) = refs[:6], refs[6:]
    loads, stores = [], []
    for j in range(6):
        buffer, out = (w.at[j], columns.at[:, pl.ds(HID * j, HID)]) if j < 4 else (d.at[j - 4], rows.at[pl.ds(HID * (j - 4), HID), :])
        loads.append(pltpu.make_async_copy(weights[j], buffer, sems.at[0, j]))
        stores.append(pltpu.make_async_copy(buffer, out, sems.at[1, j]))
    for copy in loads:
        copy.start()
    for load, store in zip(loads, stores):
        load.wait()
        store.start()
    for copy in stores:
        copy.wait()


def pack(*weights):
    scratch = [pltpu.VMEM((4, 8 * COLS, HID), BF), pltpu.VMEM((2, HID, 8 * COLS), BF), pltpu.SemaphoreType.DMA((2, 6))]
    outs = [(HBM, sds((8 * COLS, 4 * HID))), (HBM, sds((2 * HID, 8 * COLS)))]
    return call(pack_kernel, [HBM] * 6, outs, scratch, us=13, mib=MOST)(*weights)


def hidden_steps(ks, place, xs, ws, x, w, acc, sems):
    def copies(n, src):
        i = place[ks[0] + n]
        first = pltpu.make_async_copy(src, x.at[n], sems.at[1, n])
        return [first, pltpu.make_async_copy(block(ws, i), w.at[n], sems.at[0, n])]

    for n in range(len(ks)):
        for copy in copies(n, xs[n]):
            copy.start()

    @pl.loop(0, len(ks))
    def _(n):
        for copy in copies(n, xs[0]):
            copy.wait()
        acc[...] += nn(x[n], w[n])


def hidden_scratch(n):
    return [pltpu.VMEM((n, ROWS, COLS), BF), pltpu.VMEM((n, COLS, 4 * HID), BF), pltpu.SemaphoreType.DMA((2, n))]


def first_hidden_kernel(ks, place, *refs):
    n = len(ks)
    ws, acc, x, w, sems = refs[n:]
    acc[...] = jnp.zeros_like(acc)
    hidden_steps(ks, place, refs[:n], ws, x, w, acc, sems)


def first_hidden(ks, place, xs, ws):
    outs = [(VMEM, sds((ROWS, 4 * HID), F32))]
    kernel = functools.partial(first_hidden_kernel, ks)
    ins = [SMEM] + [HBM] * (len(ks) + 1)
    return call(kernel, ins, outs, hidden_scratch(len(ks)), us=8, mib=MOST)(place, *xs, ws)[0]


def dy_copies(k, ring_part, came, out, sems):
    rest = came.at[:, pl.ds(pl.multiple_of(DY_CUT + DY_REST * k, 128), DY_REST)]
    return [
        pltpu.make_async_copy(ring_part, out.at[:, pl.ds(0, DY_CUT)], sems.at[0]),
        pltpu.make_async_copy(rest, out.at[:, pl.ds(DY_CUT, DY_REST)], sems.at[1]),
    ]


def raw_steps(ks, place, dys, came, ws, dy, w, acc, sems):
    def copies(n, src):
        i = place[ks[0] + n]
        pieces = dy_copies(ks[0] + n, src, came, dy.at[n], sems.at[n])
        return pieces + [pltpu.make_async_copy(column_block(ws, i), w.at[n], sems.at[n, 2])]

    for n in range(len(ks)):
        for copy in copies(n, dys[n]):
            copy.start()

    @pl.loop(0, len(ks))
    def _(n):
        for copy in copies(n, dys[0]):
            copy.wait()
        acc[...] += nt(dy[n], w[n])


def raw_scratch(n):
    return [pltpu.VMEM((n, ROWS, COLS), BF), pltpu.VMEM((n, 2 * HID, COLS), BF), pltpu.SemaphoreType.DMA((n, 3))]


def middle_kernel(place, x_last, d0, d1, d2, came, *refs):
    ws, ds, first, keep, send, raw, acc, x, w, sems, dy, v, dsems = refs
    acc[...] = first[...]
    hidden_steps(range(3, 4), place, [x_last], ws, x, w, acc, sems)
    keep[...] = acc[:, : 2 * HID]
    send[...] = acc[:, 2 * HID :]
    raw[...] = jnp.zeros_like(raw)
    raw_steps(range(3), place, [d0, d1, d2], came, ds, dy, v, raw, dsems)


def middle(place, x_last, dys, came, ws, ds, first):
    outs = [(VMEM, sds((ROWS, 2 * HID), F32))] * 3
    scratch = [pltpu.VMEM((ROWS, 4 * HID), F32)] + hidden_scratch(1) + raw_scratch(3)
    ins = [SMEM] + [HBM] * 7 + [VMEM]
    return call(middle_kernel, ins, outs, scratch, us=12, mib=MOST)(place, x_last, *dys, came, ws, ds, first)


def activation_kernel(keep, came, s_ref, slope_ref, h_ref):
    for lo in range(0, ROWS, 128):
        rows = pl.ds(lo, 128)
        ab = keep[rows, :] + came[rows, :]
        av, bv = ab[:, :HID], ab[:, HID:]
        sig = jax.nn.sigmoid(av)
        s = av * sig
        s_ref[rows, :] = s
        h_ref[rows, :] = s * bv
        slope_ref[rows, :] = bv * sig * (1.0 + av * (1.0 - sig))


def activation(keep, came):
    return call(activation_kernel, [VMEM] * 2, [(VMEM, sds((ROWS, HID), F32))] * 3)(keep, came)


def raw_kernel(ks, place, *refs):
    n = len(ks)
    came, ws, first, keep, send, acc, dy, w, sems = refs[n:]
    acc[...] = first[...]
    raw_steps(ks, place, refs[:n], came, ws, dy, w, acc, sems)
    keep[...] = acc[:, :HID]
    send[...] = acc[:, HID:]


def raw_rest(ks, place, dys, came, ws, first):
    outs = [(VMEM, sds((ROWS, HID), F32))] * 2
    scratch = [pltpu.VMEM((ROWS, 2 * HID), F32)] + raw_scratch(len(ks))
    ins = [SMEM] + [HBM] * (len(ks) + 2) + [VMEM]
    return call(functools.partial(raw_kernel, ks), ins, outs, scratch, us=3, mib=58)(place, *dys, came, ws, first)


def gradient_kernel(keep, came, s_ref, slope_ref, h_ref, gate, dab, hs):
    sums = []
    for i in range(ROWS // 128):
        rows = pl.ds(128 * i, 128)
        g, raw, h = gate[rows, 0:1].astype(F32), keep[rows, :] + came[rows, :], h_ref[rows, :]
        value = jnp.sum(h * raw, axis=1, keepdims=True)
        sums.append(jnp.broadcast_to(value, (128, 128)).T[0:1, :])
        dh = g * raw
        dab[rows, :HID] = (dh * slope_ref[rows, :]).astype(BF)
        dab[rows, HID:] = (dh * s_ref[rows, :]).astype(BF)
        hs[rows, :] = (g * h).astype(BF)
    tail = [jnp.concatenate(sums[:4], axis=1), jnp.concatenate([sums[4], jnp.zeros((1, 384), F32)], axis=1)]
    dab[ROWS:, :] = jnp.concatenate(tail + [jnp.zeros((TAIL - 2, 512), F32)], axis=0).astype(BF)


def gradients(keep, came, s, slope, h, gate):
    outs = [(VMEM, sds((ROWS + TAIL, 2 * HID))), (VMEM, sds((ROWS, HID)))]
    return call(gradient_kernel, [VMEM] * 6, outs)(keep, came, s, slope, h, gate)


def input_kernel(k, place, own, other, *refs):
    ws, (out, w, grads, sem) = refs[0], refs[-4:]
    start = pl.multiple_of(place[k] * COLS, COLS)
    copy = pltpu.make_async_copy(ws.at[pl.ds(start, OUT_CUT), :], w, sem)
    copy.start()
    grads[:, : 2 * HID], grads[:, 2 * HID :] = own[:ROWS, :], other[:ROWS, :]
    tail = own[ROWS:, :].astype(F32) + other[ROWS:, :].astype(F32)
    row = jnp.concatenate([tail[0:1, :], tail[1:2, :128]], axis=1)
    out[ROWS:, :] = jnp.concatenate([row, jnp.zeros((TAIL - 1, OUT_CUT), F32)], axis=0).astype(BF)
    copy.wait()
    out[:ROWS, :] = nt(grads[...], w[...]).astype(BF)


def input_part(k, place, own, other, ws, *later):
    scratch = [pltpu.VMEM((OUT_CUT, 4 * HID), BF), pltpu.VMEM((ROWS, 4 * HID), BF), pltpu.SemaphoreType.DMA]
    outs = [(VMEM, sds((ROWS + TAIL, OUT_CUT)))]
    ins = [SMEM, VMEM, VMEM, HBM] + [ANY] * len(later)
    return call(functools.partial(input_kernel, k), ins, outs, scratch, us=4, mib=51)(place, own, other, ws, *later)[0]


def rest_kernel(place, own, other, ws, _, out, w, grads, sems):
    copies = []
    for k in range(4):
        start = pl.multiple_of(place[k] * COLS + OUT_CUT, 128)
        copies.append(pltpu.make_async_copy(ws.at[pl.ds(start, OUT_REST), :], w.at[k], sems.at[k]))
    for copy in copies:
        copy.start()
    grads[:, : 2 * HID], grads[:, 2 * HID :] = own[:ROWS, :], other[:ROWS, :]
    for k in range(4):
        copies[k].wait()
        out[:, OUT_REST * k : OUT_REST * k + OUT_REST] = nt(grads[...], w[k]).astype(BF)


def rest_parts(place, own, other, ws, later):
    scratch = [pltpu.VMEM((4, OUT_REST, 4 * HID), BF), pltpu.VMEM((ROWS, 4 * HID), BF), pltpu.SemaphoreType.DMA((4,))]
    outs = [(VMEM, sds((ROWS, 4 * OUT_REST)))]
    return call(rest_kernel, [SMEM, VMEM, VMEM, HBM, ANY], outs, scratch, us=4, mib=51)(place, own, other, ws, later)[0]


def stream(refs, buffer, sems):
    def load(k, src):
        return pltpu.make_async_copy(src, buffer.at[k], sems.at[k])

    for k, ref in enumerate(refs):
        load(k, ref).start()
    return lambda k: load(k, refs[0]).wait()


def dy_stream(refs, came, buffer, sems):
    for k, ref in enumerate(refs):
        for copy in dy_copies(k, ref, came, buffer.at[k], sems.at[k]):
            copy.start()

    def ready(k):
        for copy in dy_copies(k, refs[0], came, buffer.at[k], sems.at[k]):
            copy.wait()

    return ready


def other_gradient_kernel(*refs):
    xs, dys, (came, dab, hs, _, columns, rows, x, dy, c, r, xsems, dsems, sems) = refs[:4], refs[4:8], refs[8:]
    x_ready, dy_ready = stream(xs, x, xsems), dy_stream(dys, came, dy, dsems)

    def stores(k):
        return [
            pltpu.make_async_copy(c.at[k], columns.at[k], sems.at[0, k]),
            pltpu.make_async_copy(r.at[k], rows.at[k], sems.at[1, k]),
        ]

    hst = hs[...].T

    @pl.loop(0, 4)
    def _(k):
        x_ready(k)
        c[k] = tn(x[k], dab[:ROWS, :]).astype(BF)
        dy_ready(k)
        r[k] = nn(hst, dy[k]).astype(BF)
        for copy in stores(k):
            copy.start()

    @pl.loop(0, 4)
    def _(k):
        for copy in stores(k):
            copy.wait()


PIECES = [pltpu.VMEM((4, ROWS, COLS), BF)] * 2 + [pltpu.VMEM((4, COLS, 2 * HID), BF), pltpu.VMEM((4, HID, COLS), BF)]


def other_gradients(xs, dys, came, dab, hs, later):
    scratch = PIECES + [pltpu.SemaphoreType.DMA((4,)), pltpu.SemaphoreType.DMA((4, 2)), pltpu.SemaphoreType.DMA((2, 4))]
    outs = [(HBM, sds((4, COLS, 2 * HID))), (HBM, sds((4, HID, COLS)))]
    ins = [HBM] * 9 + [VMEM] * 2 + [ANY]
    return call(other_gradient_kernel, ins, outs, scratch, us=10, mib=MOST)(*xs, *dys, came, dab, hs, later)


def own_gradient_kernel(place, other_place, *refs):
    xs, dys, came, refs = refs[:4], refs[4:8], refs[8], refs[9:]
    dab, hs, columns, rows, _, g, u, d, token, x, dy, c, r, c_in, r_in, xsems, dsems, isems, sems = refs
    token[...] = jnp.zeros_like(token)
    x_ready, dy_ready = stream(xs, x, xsems), dy_stream(dys, came, dy, dsems)

    def arrivals(k):
        return [
            pltpu.make_async_copy(columns.at[k], c_in.at[k], isems.at[0, k]),
            pltpu.make_async_copy(rows.at[k], r_in.at[k], isems.at[1, k]),
        ]

    def stores(i, k, cols, part, row):
        return [
            pltpu.make_async_copy(cols.at[k, :, pl.ds(0, HID)], block(g, i), sems.at[row, k]),
            pltpu.make_async_copy(cols.at[k, :, pl.ds(HID, HID)], block(u, i), sems.at[row + 1, k]),
            pltpu.make_async_copy(part.at[k], column_block(d, i), sems.at[row + 2, k]),
        ]

    for k in range(4):
        for copy in arrivals(k):
            copy.start()
    hst = hs[...].T

    @pl.loop(0, 4)
    def _(k):
        x_ready(k)
        c[k] = tn(x[k], dab[:ROWS, :]).astype(BF)
        dy_ready(k)
        r[k] = nn(hst, dy[k]).astype(BF)
        for copy in stores(place[k], k, c, r, 0):
            copy.start()
        for copy in arrivals(k):
            copy.wait()
        for copy in stores(other_place[k], k, c_in, r_in, 3):
            copy.start()

    @pl.loop(0, 4)
    def _(k):
        for copy in stores(place[k], k, c, r, 0) + stores(other_place[k], k, c_in, r_in, 3):
            copy.wait()


def own_gradients(place, other_place, xs, dys, came, dab, hs, columns, rows, later):
    scratch = PIECES + PIECES[2:] + [pltpu.SemaphoreType.DMA((4,)), pltpu.SemaphoreType.DMA((4, 2))]
    scratch += [pltpu.SemaphoreType.DMA((2, 4)), pltpu.SemaphoreType.DMA((6, 4))]
    outs = [(HBM, sds((8 * COLS, HID)))] * 2 + [(HBM, sds((HID, 8 * COLS))), (VMEM, sds((8, 128), F32))]
    ins = [SMEM] * 2 + [HBM] * 9 + [VMEM] * 2 + [HBM] * 2 + [ANY]
    kernel = call(own_gradient_kernel, ins, outs, scratch, us=1, mib=MOST)
    return kernel(place, other_place, *xs, *dys, came, dab, hs, columns, rows, later)


def total_kernel(expert, *refs):
    terms, out = refs[:3], refs[-1]
    lane = lax.broadcasted_iota(jnp.int32, (128, PAD), 1)
    gates = sum(term[ROWS:, :].astype(F32) for term in terms)
    for i in range(ROWS // 128):
        rows = pl.ds(128 * i, 128)
        out[rows, :OUT_CUT] = sum(term[rows, :].astype(F32) for term in terms).astype(BF)
        gate = jnp.broadcast_to(gates[0:1, 128 * i : 128 * i + 128], (128, 128)).T
        high = gate.astype(BF).astype(F32)
        spread = jnp.where(lane == expert[0], high, 0.0) + jnp.where(lane == expert[0] + 64, gate - high, 0.0)
        out[rows, OUT_CUT:] = spread.astype(BF)


def total(expert, terms, *later):
    outs = [(VMEM, sds((ROWS, OUT_CUT + PAD)))]
    ins = [SMEM] + [VMEM] * 3 + [ANY] * len(later)
    return call(total_kernel, ins, outs)(expert, *terms, *later)[0]


def after(v, *later):
    return pl.pallas_call(
        lambda *refs: None,
        in_specs=[HBM] + [ANY] * len(later),
        out_specs=HBM,
        out_shape=sds(v.shape, v.dtype),
        input_output_aliases={0: 0},
    )(v, *later)


def exchange(v):
    return lax.all_to_all(v.reshape(16, ROOM, -1), ("x", "z"), 0, 0, tiled=True).reshape(ROWS, -1)


def ring(v):
    return [v, meet(v, 0), meet(v, 1)]


def add(*terms):
    return sum(term.astype(F32) for term in terms).astype(BF)


def local(tokens, cotangent, ids, gates, wg, wu, wd):
    core, iy = lax.axis_index("core"), lax.axis_index("y")
    expert = (lax.axis_index("x") * 4 + lax.axis_index("z")).astype(jnp.int32).reshape(1)
    ys = [iy, jnp.where(core == 0, iy ^ 1, 3 - iy), jnp.where(core == 0, 3 - iy, iy ^ 1), (iy + 2) % 4]
    place = jnp.stack([2 * y + core for y in ys]).astype(jnp.int32)
    other_place = jnp.stack([2 * ys[k] + 1 - core for k in (0, 2, 1, 3)]).astype(jnp.int32)
    wg, wu, wd = wg[0], wu[0], wd[0]

    send_x, onehot, weights = dispatch(ids.T, gates.T.astype(F32), tokens)
    pair = cotangent[:, DY_CUT:]
    pair = jnp.concatenate([pair, meet(pair, 0)])
    rests = [pair, meet(pair, 1)]
    send_dy = second_dispatch(onehot, weights, cotangent, rests)
    ws = (wg, wu, swap(wg), swap(wu))
    ds = (wd, swap(wd))
    xs = ring(after(exchange(send_x), ws[2], ws[3], ds[1]))
    x_last = meet(xs[1], 1)
    came = exchange(after(send_dy, xs[0]))
    gate = came[:, -PAD:]
    dys = ring(came[:, :DY_CUT])
    dys[1] = after(dys[1], dys[2])
    dy_last = meet(dys[1], 1)

    ws, ds = pack(*ws, *ds)
    first = first_hidden(range(3), place, xs, ws)
    keep, send, raw = middle(place, x_last, dys, came, ws, ds, first)
    s, slope, h = activation(keep, swap(send))
    keep, send = raw_rest(range(3, 4), place, [dy_last], came, ds, raw)
    dab, hs = gradients(keep, swap(send), s, slope, h, gate)
    dab_other, hs_other = swap(dab), swap(hs)

    def part(k, *later):
        return input_part(k, place, dab, dab_other, ws, *later)

    opposite = part(3)
    near = part(2, opposite)
    rest_back = exchange(rest_parts(place, dab, dab_other, ws, near))
    own = part(1, near)
    opposite, near = meet(opposite, 1), meet(near, 1)
    own = add(own, opposite)
    rest = meet(own, 0)
    xs, dys = xs + [x_last], dys + [dy_last]
    columns, rows = other_gradients(xs, dys, came, dab_other, hs_other, own)
    columns, rows = swap(columns), swap(rows)
    share = total(expert, (part(0, own), near, rest))
    gate_grad, up_grad, down_grad, done = own_gradients(place, other_place, xs, dys, came, dab, hs, columns, rows, share)
    ends = first_combine(rest_back, onehot, share)
    ends = ends[0] + meet(ends[1], 1)
    ends = (ends[:64], meet(ends[64:], 0))
    input_grad, slot_grad = combine(exchange(share), onehot, ids, ends, done)
    return input_grad, slot_grad, gate_grad[None], up_grad[None], down_grad[None]


def solution(mesh):
    torus = Mesh(mesh.devices.reshape(4, 4, 4, 2), ("x", "z", "y", "core"))
    ep, etp = ("x", "z"), ("y", "core")
    in_specs = (
        P(ep, etp),
        P(ep, etp),
        P(ep, None),
        P(ep, None),
        P(ep, None, etp),
        P(ep, None, etp),
        P(ep, etp, None),
    )
    out_specs = (P(ep, etp), P(ep, None), P(ep, None, etp), P(ep, None, etp), P(ep, etp, None))
    return jax.shard_map(local, mesh=torus, in_specs=in_specs, out_specs=out_specs, check_vma=False)
```
